512 devices in a mesh: gx: 16 (over z_lo, core), gy: 32 (over z_hi, y, x).
Axes of the slice: x: 4, y: 4, z: 16 (z_hi: 2, z_lo: 8; z = z_hi * 8 + z_lo), core: 2. Of those that a mesh axis runs over, the one named last changes fastest.
Arguments:
- c_upper: bfloat16 [16, 32, 96, 96], P('gx', 'gy'), may hold values from -60 to 60
- edge_upper: bfloat16 [16, 32, 96, 1536], P('gx', 'gy'), may hold values from -60 to 60
- edge_left: bfloat16 [16, 32, 96, 1536], P('gx', 'gy'), may hold values from -60 to 60
- c_lower: bfloat16 [16, 32, 96, 96], P('gx', 'gy'), may hold values from -60 to 60
- edge_lower: bfloat16 [16, 32, 96, 1536], P('gx', 'gy'), may hold values from -60 to 60
- site_ket: bfloat16 [16, 32, 2, 256], P('gx', 'gy'), may hold values from -6 to 6
- time_gate: float32 [2, 2], replicated, may hold values from -3 to 3
- quench_sites: int32 [4], replicated, may hold values from 0 to 511
Outputs:
- new_c_upper: bfloat16 [16, 32, 96, 96], P('gx', 'gy')
- new_edge_left: bfloat16 [16, 32, 96, 1536], P('gx', 'gy')
- new_c_lower: bfloat16 [16, 32, 96, 96], P('gx', 'gy')
The draws below stay inside these ranges and needn't reach their ends.
All inputs are finite; a program needn't handle non-finite values.
Results may differ from the reference program's by a relative error of at most 0.03.
Values may be sent and summed in bfloat16 or wider, within the bound.
A program may use at most 64 MiB of HBM per device.

```python
import math
import jax
import jax.numpy as jnp
from jax import lax

CHI = 96
BOND = 4
PHYS = 2
NS_ITERS = 6
STEPS = 2
QUENCH = 4
B = 16
NCOL = 16
NROW = 32


def scaled_entries(key, rows, cols):
    base_key, row_key, col_key = jax.random.split(key, 3)
    shape = (NCOL, NROW, rows, cols)
    base = jnp.clip(jax.random.normal(base_key, shape, jnp.float32), -6.0, 6.0)
    top = math.log(10.0)
    row_scale = jnp.exp(jax.random.uniform(row_key, (NCOL, NROW, rows, 1), jnp.float32, 0.0, top))
    col_scale = jnp.exp(jax.random.uniform(col_key, (NCOL, NROW, 1, cols), jnp.float32, 0.0, top))
    return (base * row_scale * col_scale * 0.1).astype(jnp.bfloat16)


def draw_c_upper(key, part):
    return scaled_entries(jax.random.fold_in(key, 11), CHI, CHI)


def draw_edge_upper(key, part):
    return scaled_entries(jax.random.fold_in(key, 12), CHI, B * CHI)


def draw_edge_left(key, part):
    return scaled_entries(jax.random.fold_in(key, 13), CHI, B * CHI)


def draw_c_lower(key, part):
    return scaled_entries(jax.random.fold_in(key, 14), CHI, CHI)


def draw_edge_lower(key, part):
    return scaled_entries(jax.random.fold_in(key, 15), CHI, B * CHI)


def place_ends(result, rng, low, high):
    place = [jax.random.randint(jax.random.fold_in(rng, axis), (), 0, length) for axis, length in enumerate(result.shape)]
    widest = result.shape.index(max(result.shape))
    neighbour = place[:widest] + [(place[widest] + 1) % result.shape[widest]] + place[widest + 1:]
    return result.at[tuple(place)].set(low).at[tuple(neighbour)].set(high)


def shard_levels(stream_key, extent, pieces, smallest, high):
    def one(axis_at, parts):
        draws = jax.random.uniform(jax.random.fold_in(jax.random.fold_in(stream_key, 6), axis_at), (parts,), jnp.float32, smallest / len(pieces), high / len(pieces))
        return jnp.repeat(jnp.exp(draws), extent[axis_at] // parts).reshape((-1,) + (1,) * (len(extent) - axis_at - 1))

    gain = one(*pieces[0])
    for cut in pieces[1:]:
        gain = gain * one(*cut)
    return gain


def normal_values(rng, shape, deviation, bound, pieces=(), kind=jnp.bfloat16):
    factor_of = shard_levels(rng, shape, pieces, -0.22, 0.18) if pieces else 1.0
    entries = jax.random.normal(rng, shape, jnp.float32) * deviation * factor_of
    return jnp.minimum(jnp.maximum(entries, -bound), bound).astype(kind)


def setup_inputs(seed: int = 0) -> dict:
    keys = jax.random.split(jax.random.key(seed), 9)
    return {
        "c_upper": draw_c_upper(jax.random.fold_in(keys[8], 71), 0),
        "edge_upper": draw_edge_upper(jax.random.fold_in(keys[8], 71), 0),
        "edge_left": draw_edge_left(jax.random.fold_in(keys[8], 71), 0),
        "c_lower": draw_c_lower(jax.random.fold_in(keys[8], 71), 0),
        "edge_lower": draw_edge_lower(jax.random.fold_in(keys[8], 71), 0),
        "site_ket": normal_values(keys[5], (NCOL, NROW, PHYS, BOND * BOND * BOND * BOND), 1.0, 6.0, ((0, 16), (1, 32))),
        "time_gate": normal_values(keys[6], (PHYS, PHYS), 1.0, 3.0, (), jnp.float32),
        "quench_sites": place_ends(jax.random.randint(keys[7], (QUENCH,), 0, NCOL * NROW), jax.random.fold_in(keys[7], 1), 0, (NCOL * NROW) - 1).astype(jnp.int32),
    }


def polar_factor(matrix):
    scale = jnp.sqrt(jnp.sum(matrix * matrix) + 1e-06)
    iterate = matrix / scale
    for sweep in range(NS_ITERS):
        gram = jnp.dot(iterate.T, iterate, precision=lax.Precision.HIGHEST)
        iterate = 1.5 * iterate - 0.5 * jnp.dot(iterate, gram, precision=lax.Precision.HIGHEST)
    return iterate

def unit_scaled(tensor):
    return tensor / jnp.sqrt(jnp.mean(tensor * tensor) + 1e-06)

def absorb_column(columns):
    corner_in, west_in, lower_in, north_edge, south_edge, ket_col, bra_col = columns
    upper = jnp.einsum('yab,ybc->yac', corner_in.astype(jnp.float32), north_edge.astype(jnp.float32)).reshape(NROW, CHI * B, CHI)
    lower = jnp.einsum('yab,ybc->yac', lower_in.astype(jnp.float32), south_edge.astype(jnp.float32)).reshape(NROW, CHI * B, CHI)
    proj_below = jax.vmap(polar_factor)(lower + jnp.roll(upper, -1, axis=0))
    proj_above = jnp.roll(proj_below, 1, axis=0)
    corner_up = jnp.einsum('yri,yrc->yic', proj_above, upper, precision=lax.Precision.HIGHEST)
    corner_low = jnp.einsum('yri,yrc->yic', proj_below, lower, precision=lax.Precision.HIGHEST)
    corner_up = jax.vmap(unit_scaled)(corner_up).astype(jnp.bfloat16)
    corner_low = jax.vmap(unit_scaled)(corner_low).astype(jnp.bfloat16)
    low_half = proj_below.astype(jnp.bfloat16).astype(jnp.float32).reshape(NROW, CHI, B, CHI)
    up_half = proj_above.astype(jnp.bfloat16).astype(jnp.float32).reshape(NROW, CHI, BOND, BOND, CHI)
    west = west_in.astype(jnp.float32).reshape(NROW, CHI, B, CHI)
    first = jnp.einsum('yulw,ywdj->yuldj', west, low_half).astype(jnp.bfloat16)
    first = first.reshape(NROW, CHI, BOND, BOND, BOND, BOND, CHI)
    second = jnp.einsum('yuaebfj,ysagcb->yuefjsgc', first.astype(jnp.float32), ket_col.astype(jnp.float32)).astype(jnp.bfloat16)
    third = jnp.einsum('yuefjsgc,ysehkf->yughckj', second.astype(jnp.float32), bra_col.astype(jnp.float32)).astype(jnp.bfloat16)
    edge_new = jnp.einsum('yughi,yughckj->yickj', up_half, third.astype(jnp.float32)).reshape(NROW, CHI, B * CHI)
    edge_new = jax.vmap(unit_scaled)(edge_new).astype(jnp.bfloat16)
    return (corner_up, edge_new, corner_low)

def reference(c_upper, edge_upper, edge_left, c_lower, edge_lower, site_ket, time_gate, quench_sites):
    ket_wide = site_ket.astype(jnp.float32).reshape(NCOL, NROW, PHYS, BOND, BOND, BOND, BOND)
    gram = jnp.dot(time_gate.T, time_gate, precision=lax.Precision.HIGHEST)
    gated = jnp.einsum('st,xytabcd->xysabcd', gram, ket_wide, precision=lax.Precision.HIGHEST)
    flat_index = (jnp.arange(NCOL, dtype=jnp.int32)[:, None] * NROW + jnp.arange(NROW, dtype=jnp.int32)[None, :]).astype(jnp.int32)
    hit_any = jnp.any(flat_index[:, :, None] == quench_sites.astype(jnp.int32)[None, None, :], axis=-1)
    chosen = hit_any[:, :, None, None, None, None, None]
    bra = jnp.where(chosen, gated, ket_wide).astype(jnp.bfloat16)
    ket_sites = site_ket.reshape(NCOL, NROW, PHYS, BOND, BOND, BOND, BOND)
    corner_up, west_edge, corner_low = (c_upper, edge_left, c_lower)
    for step in range(STEPS):
        fresh = lax.map(absorb_column, (corner_up, west_edge, corner_low, edge_upper, edge_lower, ket_sites, bra))
        corner_up = jnp.roll(fresh[0], 1, axis=0)
        west_edge = jnp.roll(fresh[1], 1, axis=0)
        corner_low = jnp.roll(fresh[2], 1, axis=0)
    return (corner_up, west_edge, corner_low)
```

```python
import jax
import jax.numpy as jnp
from jax import lax
from jax.experimental import pallas as pl
from jax.experimental.pallas import tpu as pltpu
from jax.sharding import PartitionSpec as P

NS_ITERS = 6
STEPS = 2
MESH = pl.DeviceIdType.MESH
CHI = 96
B = 16
L = 128
F32 = jnp.float32
BF = jnp.bfloat16


def nt(a, b):
    return lax.dot_general(a, b, (((1,), (1,)), ((), ())), preferred_element_type=F32)


def nn(a, b):
    return jnp.dot(a, b, preferred_element_type=F32)


def split(x):
    hi = x.astype(BF)
    return hi, (x - hi.astype(F32)).astype(BF)


def product(a, b):
    a_hi, a_lo = split(a)
    b_hi, b_lo = split(b)
    return nn(
        jnp.concatenate([a_hi, a_lo], axis=1), jnp.concatenate([b_hi, b_hi], axis=0)
    ) + nn(a_hi, b_lo)


def eye():
    row = lax.broadcasted_iota(jnp.int32, (L, L), 0)
    col = lax.broadcasted_iota(jnp.int32, (L, L), 1)
    return jnp.where((row == col) & (row < CHI), 1.0, 0.0).astype(F32)


def polar_right(grams):
    one = eye()
    scales = [1.0 / (jnp.sum(g * one) + 1e-06) for g in grams]
    ss = [g * s for g, s in zip(grams, scales)]
    ps = [1.5 * one - 0.5 * s for s in ss]
    ms = list(ps)
    for _ in range(NS_ITERS - 1):
        vs = [product(s, p) for s, p in zip(ss, ps)]
        ss = [product(v, p) for v, p in zip(vs, ps)]
        ps = [1.5 * one - 0.5 * s for s in ss]
        ms = [product(m, p) for m, p in zip(ms, ps)]
    return [m * jnp.sqrt(s) for m, s in zip(ms, scales)]


def unit_corner(x):
    return (x * lax.rsqrt(jnp.sum(x * x) * (1.0 / (CHI * CHI)) + 1e-06)).astype(BF)


def transposed_edge(edge_ref, out_ref):
    for chunk in range(4):
        lanes = edge_ref[:, chunk * 384 : (chunk + 1) * 384]
        lanes = jnp.concatenate([lanes, jnp.zeros((L - CHI, 384), BF)], axis=0)
        turned = lanes.T
        for i in range(4):
            d = chunk * 4 + i
            out_ref[d * L : d * L + CHI, :] = turned[i * CHI : (i + 1) * CHI, :]
            out_ref[d * L + CHI : (d + 1) * L, :] = jnp.zeros((L - CHI, L), BF)


def double_layer(ket_ref, gate_ref, quench_ref, own_index, out_ref):
    n = lax.broadcasted_iota(jnp.int32, (256, 256), 0)
    m = lax.broadcasted_iota(jnp.int32, (256, 256), 1)
    f4 = lambda x, k: (x >> (6 - 2 * k)) & 3
    ket_mask = (f4(n, 2) == f4(m, 1)) & (f4(n, 0) == f4(m, 2))
    bra_mask = (f4(n, 3) == f4(m, 1)) & (f4(n, 1) == f4(m, 2))
    ket_spread = ((f4(n, 0) == f4(m, 2)) & (f4(n, 3) == f4(m, 0))).astype(F32).astype(BF)
    bra_spread = ((f4(n, 0) == f4(m, 3)) & (f4(n, 3) == f4(m, 1))).astype(F32).astype(BF)
    chosen = quench_ref[0] == own_index
    for i in range(1, 4):
        chosen = chosen | (quench_ref[i] == own_index)
    kets = [ket_ref[0, 0, s : s + 1, :].astype(F32) for s in range(2)]
    total = jnp.zeros((256, 256), F32)
    for s in range(2):
        bra = jnp.zeros((1, 256), F32)
        for t in range(2):
            gram = gate_ref[0, s] * gate_ref[0, t] + gate_ref[1, s] * gate_ref[1, t]
            weight = jnp.where(chosen, gram, 1.0 if s == t else 0.0)
            bra = bra + weight * kets[t]
        bra = bra.astype(BF).astype(F32)
        ket_part = nn(jnp.where(ket_mask, kets[s], 0.0).astype(BF), ket_spread)
        bra_part = nn(jnp.where(bra_mask, bra, 0.0).astype(BF), bra_spread)
        total = total + ket_part * bra_part
    out_ref[...] = total.astype(BF)


def kernel(
    c_up_in, e_up_in, e_left_in, c_low_in, e_low_in, ket_ref, gate_ref, quench_ref,
    c_up_out, e_out, c_low_out,
    own_up, own_low, near_up, near_low, west_nat, c_in,
    et_ll, et_lu, et_ul, et_uu, cpad, c_send, c_recv, w_ref, west, west_recv, west_send,
    gt_b, lt_b, ut_b, gt_a, lt_a, ut_a, inter, pup, pt, fs, t_ref, e_fin, c_fin,
    lsem, ssem, rsem,
):
    gx, gy = lax.axis_index("gx"), lax.axis_index("gy")
    ncol, nrow = lax.axis_size("gx"), lax.axis_size("gy")
    north = (gx, lax.rem(gy + nrow - 1, nrow))
    south = (gx, lax.rem(gy + 1, nrow))
    east = (lax.rem(gx + 1, ncol), gy)
    before = (lax.rem(gx + ncol - 1, ncol), gy)
    barrier = pltpu.get_barrier_semaphore()
    for peer in (north, south, east, before):
        pl.semaphore_signal(barrier, inc=1, device_id=peer, device_id_type=MESH)

    local = [
        pltpu.make_async_copy(src.at[0, 0], dst, lsem.at[i])
        for i, (src, dst) in enumerate((
            (e_up_in, own_up), (e_low_in, own_low), (e_left_in, west_nat),
            (c_up_in, c_in.at[0]), (c_low_in, c_in.at[1]),
        ))
    ]
    for copy in local:
        copy.start()
    pl.semaphore_wait(barrier, 4)

    def remote(src, dst, i, peer):
        return pltpu.make_async_remote_copy(
            src_ref=src, dst_ref=dst, send_sem=ssem.at[i], recv_sem=rsem.at[i],
            device_id=peer, device_id_type=MESH,
        )

    first_sends = [
        remote(e_up_in.at[0, 0], near_up, 0, north),
        remote(e_low_in.at[0, 0], near_low, 1, south),
        remote(c_up_in.at[0, 0], c_in.at[2], 2, north),
        remote(c_low_in.at[0, 0], c_in.at[3], 3, south),
    ]
    for copy in first_sends:
        copy.start()

    double_layer(ket_ref, gate_ref, quench_ref, gx * nrow + gy, w_ref)
    for copy in local:
        copy.wait()
    transposed_edge(own_up, et_uu)
    transposed_edge(own_low, et_ll)
    for l in range(B):
        inter[pl.ds(l, CHI, stride=B), :] = jnp.concatenate(
            [west_nat[:, l * CHI : (l + 1) * CHI].astype(F32), jnp.zeros((CHI, L - CHI), F32)], axis=1
        )
    west[...] = inter[...].astype(BF)

    for copy in first_sends:
        copy.wait_recv()
    for slot, place in enumerate((1, 2, 3, 0)):
        cpad[slot] = jnp.zeros((L, L), BF)
        cpad[slot, 0:CHI, :] = jnp.concatenate([c_in[place], jnp.zeros((CHI, L - CHI), BF)], axis=1)
    transposed_edge(near_up, et_lu)
    transposed_edge(near_low, et_ul)

    for step in range(STEPS):
        corners = cpad if step == 0 else c_recv
        if step > 0:
            remote(c_send, c_recv, 4, east).wait_recv()
        cuts = ((et_ll, et_lu, 0, 1, gt_b, lt_b, ut_b), (et_ul, et_uu, 2, 3, gt_a, lt_a, ut_a))
        grams, rows_low, rows_up = [], [], []
        for et_low, et_up, i_low, i_up, gt, lt, ut in cuts:
            for piece in range(8):
                rows = slice(piece * 256, (piece + 1) * 256)
                low = nt(et_low[rows, :], corners[i_low])
                up = nt(et_up[rows, :], corners[i_up])
                gt[rows, :] = (low + up).astype(BF)
                lt[rows, :] = low.astype(BF)
                ut[rows, :] = up.astype(BF)
            total = jnp.zeros((L, 3 * L), F32)
            for d in range(B):
                rows = slice(d * L, (d + 1) * L)
                right = jnp.concatenate([gt[rows, :], lt[rows, :], ut[rows, :]], axis=0)
                total = total + nt(gt[rows, :], right)
            grams.append(total[:, 0:L])
            rows_low.append(total[:, L : 2 * L])
            rows_up.append(total[:, 2 * L : 3 * L])
        for up in range(B):
            rows = slice(up * L, (up + 1) * L)
            value = nt(corners[2], et_ul[rows, :]) + nt(corners[3], et_uu[rows, :])
            inter[pl.ds(up, CHI, stride=B), :] = value[0:CHI, :]
        m_b, m_a = polar_right(grams)
        new_low_b = unit_corner(product(m_b, rows_low[0]))
        new_up_a = unit_corner(product(m_a, rows_up[1]))
        if step < STEPS - 1:
            c_send[0] = new_low_b
            c_send[1] = unit_corner(product(m_b, rows_up[0]))
            c_send[2] = unit_corner(product(m_a, rows_low[1]))
            c_send[3] = new_up_a
            corner_sends = [remote(c_send, c_recv, 4, east)]
        else:
            c_fin[0] = new_up_a[0:CHI, 0:CHI]
            c_fin[1] = new_low_b[0:CHI, 0:CHI]
            corner_sends = [
                remote(c_fin.at[0], c_up_out.at[0, 0], 5, east),
                remote(c_fin.at[1], c_low_out.at[0, 0], 6, east),
            ]
        for copy in corner_sends:
            copy.start()

        m_rows = jnp.concatenate(list(split(m_b)), axis=0)
        for d in range(B):
            rows = slice(d * L, (d + 1) * L)
            both = nn(m_rows, gt_b[rows, :])
            pt[rows, :] = (both[0:L] + both[L : 2 * L]).astype(BF)
        m_rows = jnp.concatenate(list(split(m_a)), axis=0)
        for piece in range(6):
            rows = slice(piece * 256, (piece + 1) * 256)
            both = nt(m_rows, inter[rows, :].astype(BF))
            pup[:, rows] = (both[0:CHI] + both[L : L + CHI]).astype(BF)

        if step > 0:
            remote(west_send, west_recv, 7, east).wait_recv()
        left = west if step == 0 else west_recv

        def block(i, carry):
            base = pl.multiple_of(i * 256, 256)
            rows = left[pl.ds(base, 256), :]
            for pair in range(8):
                out = nt(rows, pt[pair * 256 : (pair + 1) * 256, :]).astype(BF)
                fs[2 * pair] = out[:, 0:L]
                fs[2 * pair + 1] = out[:, L : 2 * L]
            for pair in range(8):
                cols = [
                    jnp.concatenate([fs[d, u * B : (u + 1) * B, :] for d in range(B)], axis=0)
                    for u in (2 * pair, 2 * pair + 1)
                ]
                out = nn(w_ref[...], jnp.concatenate(cols, axis=1)).astype(BF)
                for half in range(2):
                    at = pl.ds(pl.multiple_of(base + (2 * pair + half) * B, B), B)
                    for r in range(B):
                        t_ref[r // 2, at, (r % 2) * L : (r % 2 + 1) * L] = out[
                            r * B : (r + 1) * B, half * L : (half + 1) * L
                        ]
            return carry

        lax.fori_loop(0, 6, block, 0)

        square = jnp.zeros((CHI, CHI), F32)
        blocks = []
        for pair in range(8):
            out = nn(pup[...], t_ref[pair])
            for half in range(2):
                value = out[:, half * L : half * L + CHI]
                square = square + value * value
                r = 2 * pair + half
                if step < STEPS - 1:
                    inter[pl.ds(r, CHI, stride=B), :] = jnp.concatenate(
                        [value, jnp.zeros((CHI, L - CHI), F32)], axis=1
                    )
                else:
                    blocks.append(value)
        scale = lax.rsqrt(jnp.sum(square) * (1.0 / (CHI * CHI * B)) + 1e-06)
        if step < STEPS - 1:
            west_send[...] = (inter[...] * scale).astype(BF)
            edge_send = remote(west_send, west_recv, 7, east)
        else:
            e_fin[...] = jnp.concatenate([(v * scale).astype(BF) for v in blocks], axis=1)
            edge_send = remote(e_fin, e_out.at[0, 0], 8, east)
        edge_send.start()
        if step == STEPS - 1:
            for copy in corner_sends + [edge_send]:
                copy.wait_recv()
            for copy in corner_sends + [edge_send] + first_sends:
                copy.wait_send()
            remote(c_send, c_recv, 4, east).wait_send()
            remote(west_send, west_recv, 7, east).wait_send()


def per_device(c_upper, edge_upper, edge_left, c_lower, edge_lower, site_ket, time_gate, quench_sites):
    hbm = pl.BlockSpec(memory_space=pl.ANY)
    vmem = pl.BlockSpec(memory_space=pltpu.VMEM)
    smem = pl.BlockSpec(memory_space=pltpu.SMEM)
    corner = jax.ShapeDtypeStruct((1, 1, CHI, CHI), BF)
    edge = jax.ShapeDtypeStruct((1, 1, CHI, B * CHI), BF)
    natural = pltpu.VMEM((CHI, B * CHI), BF)
    tall = pltpu.VMEM((B * L, L), BF)
    inner = pltpu.VMEM((CHI * B, L), BF)
    four = pltpu.VMEM((4, L, L), BF)
    return pl.pallas_call(
        kernel,
        out_shape=(corner, edge, corner),
        in_specs=[hbm] * 5 + [vmem, smem, smem],
        out_specs=(hbm,) * 3,
        scratch_shapes=[
            natural, natural, natural, natural, natural, pltpu.VMEM((4, CHI, CHI), BF),
            tall, tall, tall, tall, four, four, four, pltpu.VMEM((256, 256), BF), inner, inner, inner,
            tall, tall, tall, tall, tall, tall, pltpu.VMEM((CHI * B, L), F32),
            pltpu.VMEM((CHI, CHI * B), BF), tall, pltpu.VMEM((B, 256, L), BF),
            pltpu.VMEM((8, CHI * B, 2 * L), BF), natural, pltpu.VMEM((2, CHI, CHI), BF),
            pltpu.SemaphoreType.DMA((5,)), pltpu.SemaphoreType.DMA((9,)), pltpu.SemaphoreType.DMA((9,)),
        ],
        compiler_params=pltpu.CompilerParams(
            collective_id=0, has_side_effects=True, vmem_limit_bytes=63 * 1024 * 1024
        ),
        name="left_move",
    )(c_upper, edge_upper, edge_left, c_lower, edge_lower, site_ket, time_gate, quench_sites)


def solution(mesh):
    site = P("gx", "gy", None, None)
    return jax.shard_map(
        per_device,
        mesh=mesh,
        in_specs=(site,) * 6 + (P(), P()),
        out_specs=(site,) * 3,
        check_vma=False,
    )
```

```python
import jax
import jax.numpy as jnp
from jax import lax
from jax.experimental import pallas as pl
from jax.experimental.pallas import tpu as pltpu
from jax.sharding import PartitionSpec as P

NS_ITERS = 6
STEPS = 2
MESH = pl.DeviceIdType.MESH
CHI = 96
B = 16
HALF = 16
CHUNKS = 12
L = 128
F32 = jnp.float32
BF = jnp.bfloat16


def nt(a, b):
    return lax.dot_general(a, b, (((1,), (1,)), ((), ())), preferred_element_type=F32)


def nn(a, b):
    return jnp.dot(a, b, preferred_element_type=F32)


def split(x):
    hi = x.astype(BF)
    return hi, (x - hi.astype(F32)).astype(BF)


def product(a, b):
    a_hi, a_lo = split(a)
    b_hi, b_lo = split(b)
    return nn(
        jnp.concatenate([a_hi, a_lo], axis=1), jnp.concatenate([b_hi, b_hi], axis=0)
    ) + nn(a_hi, b_lo)


def eye():
    row = lax.broadcasted_iota(jnp.int32, (L, L), 0)
    col = lax.broadcasted_iota(jnp.int32, (L, L), 1)
    return jnp.where((row == col) & (row < CHI), 1.0, 0.0).astype(F32)


def polar_right(grams):
    one = eye()
    scales = [1.0 / (jnp.sum(g * one) + 1e-06) for g in grams]
    ss = [g * s for g, s in zip(grams, scales)]
    ps = [1.5 * one - 0.5 * s for s in ss]
    ms = list(ps)
    for _ in range(NS_ITERS - 1):
        vs = [product(s, p) for s, p in zip(ss, ps)]
        ss = [product(v, p) for v, p in zip(vs, ps)]
        ps = [1.5 * one - 0.5 * s for s in ss]
        ms = [product(m, p) for m, p in zip(ms, ps)]
    return [m * jnp.sqrt(s) for m, s in zip(ms, scales)]


def unit_corner(x):
    return (x * lax.rsqrt(jnp.sum(x * x) * (1.0 / (CHI * CHI)) + 1e-06)).astype(BF)


def transposed_edge(edge_ref, out_ref):
    for chunk in range(4):
        lanes = edge_ref[:, chunk * 384 : (chunk + 1) * 384]
        lanes = jnp.concatenate([lanes, jnp.zeros((L - CHI, 384), BF)], axis=0)
        turned = lanes.T
        for i in range(4):
            d = chunk * 4 + i
            out_ref[d * L : d * L + CHI, :] = turned[i * CHI : (i + 1) * CHI, :]
            out_ref[d * L + CHI : (d + 1) * L, :] = jnp.zeros((L - CHI, L), BF)


def double_layer(ket_ref, gate_ref, quench_ref, own_index, out_ref):
    n = lax.broadcasted_iota(jnp.int32, (256, 256), 0)
    m = lax.broadcasted_iota(jnp.int32, (256, 256), 1)
    f4 = lambda x, k: (x >> (6 - 2 * k)) & 3
    ket_mask = (f4(n, 2) == f4(m, 1)) & (f4(n, 0) == f4(m, 2))
    bra_mask = (f4(n, 3) == f4(m, 1)) & (f4(n, 1) == f4(m, 2))
    ket_spread = ((f4(n, 0) == f4(m, 2)) & (f4(n, 3) == f4(m, 0))).astype(F32).astype(BF)
    bra_spread = ((f4(n, 0) == f4(m, 3)) & (f4(n, 3) == f4(m, 1))).astype(F32).astype(BF)
    chosen = quench_ref[0] == own_index
    for i in range(1, 4):
        chosen = chosen | (quench_ref[i] == own_index)
    kets = [ket_ref[0, 0, s : s + 1, :].astype(F32) for s in range(2)]
    total = jnp.zeros((256, 256), F32)
    for s in range(2):
        bra = jnp.zeros((1, 256), F32)
        for t in range(2):
            gram = gate_ref[0, s] * gate_ref[0, t] + gate_ref[1, s] * gate_ref[1, t]
            weight = jnp.where(chosen, gram, 1.0 if s == t else 0.0)
            bra = bra + weight * kets[t]
        bra = bra.astype(BF).astype(F32)
        ket_part = nn(jnp.where(ket_mask, kets[s], 0.0).astype(BF), ket_spread)
        bra_part = nn(jnp.where(bra_mask, bra, 0.0).astype(BF), bra_spread)
        total = total + ket_part * bra_part
    out_ref[...] = total.astype(BF)


def kernel(
    c_up_in, e_up_in, e_left_in, c_low_in, e_low_in, ket_ref, gate_ref, quench_ref,
    c_up_out, e_out, c_low_out,
    own_up, own_low, near_up, near_low, west_nat, c_in,
    et_ll, et_lu, et_ul, et_uu, cpad, c_send, c_recv, w_ref, west, west_recv, west_send,
    gt_b, lt_b, ut_b, gt_a, lt_a, ut_a, inter, pup, pt, fs, t_ref, e_fin, c_fin,
    hop, lsem, ssem, rsem, psem, hsem,
):
    gx, gy = lax.axis_index("gx"), lax.axis_index("gy")
    ncol, nrow = lax.axis_size("gx"), lax.axis_size("gy")
    north = (gx, lax.rem(gy + nrow - 1, nrow))
    south = (gx, lax.rem(gy + 1, nrow))
    east = (lax.rem(gx + 1, ncol), gy)
    before = (lax.rem(gx + ncol - 1, ncol), gy)
    half, place = gy // HALF, lax.rem(gy, HALF)
    spread = nrow == 2 * HALF
    first, last = place == 0, place == HALF - 1
    helper = (place >= 2) & (place < 2 + CHUNKS)
    barrier = pltpu.get_barrier_semaphore()

    def greet(peer):
        pl.semaphore_signal(barrier, inc=1, device_id=peer, device_id_type=MESH)

    for peer in (north, south, east, before):
        greet(peer)
    greeted = 4
    if spread:
        @pl.when(first | last)
        def _():
            for c in range(CHUNKS):
                greet((gx, 2 + c))
                greet((gx, HALF + 2 + c))

        @pl.when(helper)
        def _():
            for row in (0, HALF - 1, HALF, 2 * HALF - 1):
                greet((gx, row))

        greeted = 4 + jnp.where(helper, 4, 0) + jnp.where(first | last, 2 * CHUNKS, 0)

    local = [
        pltpu.make_async_copy(src.at[0, 0], dst, lsem.at[i])
        for i, (src, dst) in enumerate((
            (e_up_in, own_up), (e_low_in, own_low), (e_left_in, west_nat),
            (c_up_in, c_in.at[0]), (c_low_in, c_in.at[1]),
        ))
    ]
    for copy in local:
        copy.start()
    pl.semaphore_wait(barrier, greeted)

    def remote(src, dst, i, peer):
        return pltpu.make_async_remote_copy(
            src_ref=src, dst_ref=dst, send_sem=ssem.at[i], recv_sem=rsem.at[i],
            device_id=peer, device_id_type=MESH,
        )

    first_sends = [
        remote(e_up_in.at[0, 0], near_up, 0, north),
        remote(e_low_in.at[0, 0], near_low, 1, south),
        remote(c_up_in.at[0, 0], c_in.at[2], 2, north),
        remote(c_low_in.at[0, 0], c_in.at[3], 3, south),
    ]
    def relay(src, dst, send, recv, peer):
        return pltpu.make_async_remote_copy(
            src_ref=src, dst_ref=dst, send_sem=psem.at[send], recv_sem=recv,
            device_id=peer, device_id_type=MESH,
        )

    def chunk_sends(edge_in, slot):
        return [
            relay(edge_in.at[0, 0, :, pl.ds(c * L, L)], hop.at[slot], c, hsem.at[slot], (gx, half * HALF + 2 + c))
            for c in range(CHUNKS)
        ]

    lanes = pl.ds(pl.multiple_of((place - 2) * L, L), L)
    forwards = [
        relay(hop.at[0], near_up.at[:, lanes], 0, rsem.at[0], (gx, (1 - half) * HALF + HALF - 1)),
        relay(hop.at[1], near_low.at[:, lanes], 1, rsem.at[1], (gx, (1 - half) * HALF)),
    ]
    if spread:
        @pl.when(first)
        def _():
            for copy in chunk_sends(e_up_in, 0):
                copy.start()

        @pl.when(last)
        def _():
            for copy in chunk_sends(e_low_in, 1):
                copy.start()

        @pl.when(jnp.logical_not(first))
        def _():
            first_sends[0].start()

        @pl.when(jnp.logical_not(last))
        def _():
            first_sends[1].start()
    else:
        first_sends[0].start()
        first_sends[1].start()
    first_sends[2].start()
    first_sends[3].start()
    if spread:
        @pl.when(helper)
        def _():
            for slot in (0, 1):
                relay(hop.at[slot], hop.at[slot], slot, hsem.at[slot], north).wait_recv()
                forwards[slot].start()

    double_layer(ket_ref, gate_ref, quench_ref, gx * nrow + gy, w_ref)
    for copy in local:
        copy.wait()
    transposed_edge(own_up, et_uu)
    transposed_edge(own_low, et_ll)
    for l in range(B):
        inter[pl.ds(l, CHI, stride=B), :] = jnp.concatenate(
            [west_nat[:, l * CHI : (l + 1) * CHI].astype(F32), jnp.zeros((CHI, L - CHI), F32)], axis=1
        )
    west[...] = inter[...].astype(BF)

    for copy in first_sends:
        copy.wait_recv()
    for slot, place in enumerate((1, 2, 3, 0)):
        cpad[slot] = jnp.zeros((L, L), BF)
        cpad[slot, 0:CHI, :] = jnp.concatenate([c_in[place], jnp.zeros((CHI, L - CHI), BF)], axis=1)
    transposed_edge(near_up, et_lu)
    transposed_edge(near_low, et_ul)

    for step in range(STEPS):
        corners = cpad if step == 0 else c_recv
        if step > 0:
            remote(c_send, c_recv, 4, east).wait_recv()
        cuts = ((et_ll, et_lu, 0, 1, gt_b, lt_b, ut_b), (et_ul, et_uu, 2, 3, gt_a, lt_a, ut_a))
        grams, rows_low, rows_up = [], [], []
        for et_low, et_up, i_low, i_up, gt, lt, ut in cuts:
            for piece in range(8):
                rows = slice(piece * 256, (piece + 1) * 256)
                low = nt(et_low[rows, :], corners[i_low])
                up = nt(et_up[rows, :], corners[i_up])
                gt[rows, :] = (low + up).astype(BF)
                lt[rows, :] = low.astype(BF)
                ut[rows, :] = up.astype(BF)
            total = jnp.zeros((L, 3 * L), F32)
            for d in range(B):
                rows = slice(d * L, (d + 1) * L)
                right = jnp.concatenate([gt[rows, :], lt[rows, :], ut[rows, :]], axis=0)
                total = total + nt(gt[rows, :], right)
            grams.append(total[:, 0:L])
            rows_low.append(total[:, L : 2 * L])
            rows_up.append(total[:, 2 * L : 3 * L])
        for up in range(B):
            rows = slice(up * L, (up + 1) * L)
            value = nt(corners[2], et_ul[rows, :]) + nt(corners[3], et_uu[rows, :])
            inter[pl.ds(up, CHI, stride=B), :] = value[0:CHI, :]
        m_b, m_a = polar_right(grams)
        new_low_b = unit_corner(product(m_b, rows_low[0]))
        new_up_a = unit_corner(product(m_a, rows_up[1]))
        if step < STEPS - 1:
            c_send[0] = new_low_b
            c_send[1] = unit_corner(product(m_b, rows_up[0]))
            c_send[2] = unit_corner(product(m_a, rows_low[1]))
            c_send[3] = new_up_a
            corner_sends = [remote(c_send, c_recv, 4, east)]
        else:
            c_fin[0] = new_up_a[0:CHI, 0:CHI]
            c_fin[1] = new_low_b[0:CHI, 0:CHI]
            corner_sends = [
                remote(c_fin.at[0], c_up_out.at[0, 0], 5, east),
                remote(c_fin.at[1], c_low_out.at[0, 0], 6, east),
            ]
        for copy in corner_sends:
            copy.start()

        m_rows = jnp.concatenate(list(split(m_b)), axis=0)
        for d in range(B):
            rows = slice(d * L, (d + 1) * L)
            both = nn(m_rows, gt_b[rows, :])
            pt[rows, :] = (both[0:L] + both[L : 2 * L]).astype(BF)
        m_rows = jnp.concatenate(list(split(m_a)), axis=0)
        for piece in range(6):
            rows = slice(piece * 256, (piece + 1) * 256)
            both = nt(m_rows, inter[rows, :].astype(BF))
            pup[:, rows] = (both[0:CHI] + both[L : L + CHI]).astype(BF)

        if step > 0:
            remote(west_send, west_recv, 7, east).wait_recv()
        left = west if step == 0 else west_recv

        def spread_rows(k):
            rows = left[k * 256 : (k + 1) * 256, :]
            for pair in range(8):
                out = nt(rows, pt[pair * 256 : (pair + 1) * 256, :]).astype(BF)
                fs[k, 2 * pair] = out[:, 0:L]
                fs[k, 2 * pair + 1] = out[:, L : 2 * L]

        def absorb(k):
            for pair in range(8):
                cols = [
                    jnp.concatenate([fs[k, d, u * B : (u + 1) * B, :] for d in range(B)], axis=0)
                    for u in (2 * pair, 2 * pair + 1)
                ]
                out = nn(w_ref[...], jnp.concatenate(cols, axis=1)).astype(BF)
                for side in range(2):
                    at = k * 256 + (2 * pair + side) * B
                    for r in range(B):
                        t_ref[r // 2, at : at + B, (r % 2) * L : (r % 2 + 1) * L] = out[
                            r * B : (r + 1) * B, side * L : (side + 1) * L
                        ]

        spread_rows(0)
        for k in range(6):
            if k < 5:
                spread_rows(k + 1)
            absorb(k)

        square = jnp.zeros((CHI, CHI), F32)
        blocks = []
        for pair in range(8):
            out = nn(pup[...], t_ref[pair])
            for half in range(2):
                value = out[:, half * L : half * L + CHI]
                square = square + value * value
                r = 2 * pair + half
                if step < STEPS - 1:
                    inter[pl.ds(r, CHI, stride=B), :] = jnp.concatenate(
                        [value, jnp.zeros((CHI, L - CHI), F32)], axis=1
                    )
                else:
                    blocks.append(value)
        scale = lax.rsqrt(jnp.sum(square) * (1.0 / (CHI * CHI * B)) + 1e-06)
        if step < STEPS - 1:
            west_send[...] = (inter[...] * scale).astype(BF)
            edge_send = remote(west_send, west_recv, 7, east)
        else:
            e_fin[...] = jnp.concatenate([(v * scale).astype(BF) for v in blocks], axis=1)
            edge_send = remote(e_fin, e_out.at[0, 0], 8, east)
        edge_send.start()
        if step == STEPS - 1:
            for copy in corner_sends + [edge_send]:
                copy.wait_recv()
            for copy in corner_sends + [edge_send] + first_sends[2:]:
                copy.wait_send()
            if spread:
                @pl.when(first)
                def _():
                    for copy in chunk_sends(e_up_in, 0):
                        copy.wait_send()

                @pl.when(last)
                def _():
                    for copy in chunk_sends(e_low_in, 1):
                        copy.wait_send()

                @pl.when(jnp.logical_not(first))
                def _():
                    first_sends[0].wait_send()

                @pl.when(jnp.logical_not(last))
                def _():
                    first_sends[1].wait_send()

                @pl.when(helper)
                def _():
                    for copy in forwards:
                        copy.wait_send()
            else:
                first_sends[0].wait_send()
                first_sends[1].wait_send()
            remote(c_send, c_recv, 4, east).wait_send()
            remote(west_send, west_recv, 7, east).wait_send()


def per_device(c_upper, edge_upper, edge_left, c_lower, edge_lower, site_ket, time_gate, quench_sites):
    hbm = pl.BlockSpec(memory_space=pl.ANY)
    vmem = pl.BlockSpec(memory_space=pltpu.VMEM)
    smem = pl.BlockSpec(memory_space=pltpu.SMEM)
    corner = jax.ShapeDtypeStruct((1, 1, CHI, CHI), BF)
    edge = jax.ShapeDtypeStruct((1, 1, CHI, B * CHI), BF)
    natural = pltpu.VMEM((CHI, B * CHI), BF)
    tall = pltpu.VMEM((B * L, L), BF)
    inner = pltpu.VMEM((CHI * B, L), BF)
    four = pltpu.VMEM((4, L, L), BF)
    return pl.pallas_call(
        kernel,
        out_shape=(corner, edge, corner),
        in_specs=[hbm] * 5 + [vmem, smem, smem],
        out_specs=(hbm,) * 3,
        scratch_shapes=[
            natural, natural, natural, natural, natural, pltpu.VMEM((4, CHI, CHI), BF),
            tall, tall, tall, tall, four, four, four, pltpu.VMEM((256, 256), BF), inner, inner, inner,
            tall, tall, tall, tall, tall, tall, pltpu.VMEM((CHI * B, L), F32),
            pltpu.VMEM((CHI, CHI * B), BF), tall, pltpu.VMEM((6, B, 256, L), BF),
            pltpu.VMEM((8, CHI * B, 2 * L), BF), natural, pltpu.VMEM((2, CHI, CHI), BF),
            pltpu.VMEM((2, CHI, L), BF),
            pltpu.SemaphoreType.DMA((5,)), pltpu.SemaphoreType.DMA((9,)), pltpu.SemaphoreType.DMA((9,)),
            pltpu.SemaphoreType.DMA((CHUNKS,)), pltpu.SemaphoreType.DMA((2,)),
        ],
        compiler_params=pltpu.CompilerParams(
            collective_id=0, has_side_effects=True, vmem_limit_bytes=63 * 1024 * 1024
        ),
        name="left_move",
    )(c_upper, edge_upper, edge_left, c_lower, edge_lower, site_ket, time_gate, quench_sites)


def solution(mesh):
    site = P("gx", "gy", None, None)
    return jax.shard_map(
        per_device,
        mesh=mesh,
        in_specs=(site,) * 6 + (P(), P()),
        out_specs=(site,) * 3,
        check_vma=False,
    )
```

```python
import jax
import jax.numpy as jnp
from jax import lax
from jax.experimental import pallas as pl
from jax.experimental.pallas import tpu as pltpu
from jax.sharding import PartitionSpec as P

NS_ITERS = 6
STEPS = 2
MESH = pl.DeviceIdType.MESH
CHI = 96
B = 16
HALF = 16
CHUNKS = 12
L = 128
F32 = jnp.float32
BF = jnp.bfloat16


def nt(a, b):
    return lax.dot_general(a, b, (((1,), (1,)), ((), ())), preferred_element_type=F32)


def nn(a, b):
    return jnp.dot(a, b, preferred_element_type=F32)


def split(x):
    hi = x.astype(BF)
    return hi, (x - hi.astype(F32)).astype(BF)


def product(a, b):
    a_hi, a_lo = split(a)
    b_hi, b_lo = split(b)
    return nn(
        jnp.concatenate([a_hi, a_lo], axis=1), jnp.concatenate([b_hi, b_hi], axis=0)
    ) + nn(a_hi, b_lo)


def eye():
    row = lax.broadcasted_iota(jnp.int32, (L, L), 0)
    col = lax.broadcasted_iota(jnp.int32, (L, L), 1)
    return jnp.where((row == col) & (row < CHI), 1.0, 0.0).astype(F32)


def polar_right(gram):
    one = eye()
    scale = 1.0 / (jnp.sum(gram * one) + 1e-06)
    s = gram * scale
    p = 1.5 * one - 0.5 * s
    m = p
    for _ in range(NS_ITERS - 1):
        s = product(product(s, p), p)
        p = 1.5 * one - 0.5 * s
        m = product(m, p)
    return m * jnp.sqrt(scale)


def unit_corner(x):
    return (x * lax.rsqrt(jnp.sum(x * x) * (1.0 / (CHI * CHI)) + 1e-06)).astype(BF)


def transposed_edge(edge_ref, out_ref):
    for chunk in range(4):
        lanes = edge_ref[:, chunk * 384 : (chunk + 1) * 384]
        lanes = jnp.concatenate([lanes, jnp.zeros((L - CHI, 384), BF)], axis=0)
        turned = lanes.T
        for i in range(4):
            d = chunk * 4 + i
            out_ref[d * L : d * L + CHI, :] = turned[i * CHI : (i + 1) * CHI, :]
            out_ref[d * L + CHI : (d + 1) * L, :] = jnp.zeros((L - CHI, L), BF)


def double_layer(ket_ref, gate_ref, quench_ref, own_index, mirror, out_ref):
    n = lax.broadcasted_iota(jnp.int32, (256, 256), 0)
    m = lax.broadcasted_iota(jnp.int32, (256, 256), 1)
    f4 = lambda x, k: (x >> (6 - 2 * k)) & 3
    outer = jnp.where(mirror, f4(m, 3), f4(m, 1))
    inner = jnp.where(mirror, f4(n, 1), f4(n, 3))
    ket_mask = (f4(n, 2) == outer) & (f4(n, 0) == f4(m, 2))
    bra_mask = (f4(n, 3) == outer) & (f4(n, 1) == f4(m, 2))
    ket_spread = ((f4(n, 0) == f4(m, 2)) & (inner == f4(m, 0))).astype(F32).astype(BF)
    bra_spread = ((f4(n, 0) == f4(m, 3)) & (inner == f4(m, 1))).astype(F32).astype(BF)
    chosen = quench_ref[0] == own_index
    for i in range(1, 4):
        chosen = chosen | (quench_ref[i] == own_index)
    kets = [ket_ref[0, 0, s : s + 1, :].astype(F32) for s in range(2)]
    total = jnp.zeros((256, 256), F32)
    for s in range(2):
        bra = jnp.zeros((1, 256), F32)
        for t in range(2):
            gram = gate_ref[0, s] * gate_ref[0, t] + gate_ref[1, s] * gate_ref[1, t]
            weight = jnp.where(chosen, gram, 1.0 if s == t else 0.0)
            bra = bra + weight * kets[t]
        bra = bra.astype(BF).astype(F32)
        ket_part = nn(jnp.where(ket_mask, kets[s], 0.0).astype(BF), ket_spread)
        bra_part = nn(jnp.where(bra_mask, bra, 0.0).astype(BF), bra_spread)
        total = total + ket_part * bra_part
    out_ref[...] = total.astype(BF)


def kernel(
    c_up_in, e_up_in, e_left_in, c_low_in, e_low_in, ket_ref, gate_ref, quench_ref,
    c_up_out, e_out, c_low_out,
    own, near, west_nat, c_in, et_own, et_near, cpad, c_send, c_recv, w_ref,
    west, west_recv, west_send, glu, inter, pup, pt, fs, t_ref, fin, e_fin, c_fin,
    hop, lsem, ssem, rsem, psem, hsem,
):
    gx, gy = lax.axis_index("gx"), lax.axis_index("gy")
    ncol, nrow = lax.axis_size("gx"), lax.axis_size("gy")
    north = (gx, lax.rem(gy + nrow - 1, nrow))
    south = (gx, lax.rem(gy + 1, nrow))
    east = (lax.rem(gx + 1, ncol), gy)
    before = (lax.rem(gx + ncol - 1, ncol), gy)
    spread = nrow == 2 * HALF
    period = HALF if spread else nrow
    half, place = gy // period, lax.rem(gy, period)
    first, last = place == 0, place == period - 1
    helper = (place >= 2) & (place < 2 + CHUNKS)
    mirror = last
    flip = jnp.where(mirror, 1, 0)
    barrier = pltpu.get_barrier_semaphore()

    def greet(peer):
        pl.semaphore_signal(barrier, inc=1, device_id=peer, device_id_type=MESH)

    for peer in (north, south, east, before):
        greet(peer)
    greeted = 4
    if spread:
        @pl.when(first | last)
        def _():
            for c in range(CHUNKS):
                greet((gx, 2 + c))
                greet((gx, HALF + 2 + c))

        @pl.when(helper)
        def _():
            for row in (0, HALF - 1, HALF, 2 * HALF - 1):
                greet((gx, row))

        greeted = 4 + jnp.where(helper, 4, 0) + jnp.where(first | last, 2 * CHUNKS, 0)

    local = [
        pltpu.make_async_copy(src.at[0, 0], dst, lsem.at[i])
        for i, (src, dst) in enumerate((
            (e_low_in, own.at[flip]), (e_up_in, own.at[1 - flip]), (e_left_in, west_nat),
            (c_low_in, c_in.at[2 * flip]), (c_up_in, c_in.at[2 - 2 * flip]),
        ))
    ]
    for copy in local:
        copy.start()
    pl.semaphore_wait(barrier, greeted)

    def remote(src, dst, i, peer, j=None):
        return pltpu.make_async_remote_copy(
            src_ref=src, dst_ref=dst, send_sem=ssem.at[i], recv_sem=rsem.at[i if j is None else j],
            device_id=peer, device_id_type=MESH,
        )

    to_north = jnp.where(first, 1, 0)
    to_south = jnp.where(place == period - 2, 0, 1)
    first_sends = [
        remote(e_up_in.at[0, 0], near.at[to_north], 0, north, to_north),
        remote(e_low_in.at[0, 0], near.at[to_south], 1, south, to_south),
        remote(c_up_in.at[0, 0], c_in.at[1 + 2 * to_north], 2, north, 2 + to_north),
        remote(c_low_in.at[0, 0], c_in.at[1 + 2 * to_south], 3, south, 2 + to_south),
    ]

    def relay(src, dst, send, recv, peer):
        return pltpu.make_async_remote_copy(
            src_ref=src, dst_ref=dst, send_sem=psem.at[send], recv_sem=recv,
            device_id=peer, device_id_type=MESH,
        )

    def chunk_sends(edge_in, slot):
        return [
            relay(edge_in.at[0, 0, :, pl.ds(c * L, L)], hop.at[slot], c, hsem.at[slot], (gx, half * HALF + 2 + c))
            for c in range(CHUNKS)
        ]

    lanes = pl.ds(pl.multiple_of((place - 2) * L, L), L)

    def forwards():
        return [
            relay(hop.at[0], near.at[1, :, lanes], 0, rsem.at[1], (gx, (1 - half) * HALF + HALF - 1)),
            relay(hop.at[1], near.at[1, :, lanes], 1, rsem.at[1], (gx, (1 - half) * HALF)),
        ]

    def forward():
        for slot, copy in enumerate(forwards()):
            relay(hop.at[slot], hop.at[slot], slot, hsem.at[slot], north).wait_recv()
            copy.start()

    if spread:
        @pl.when(first)
        def _():
            for copy in chunk_sends(e_up_in, 0):
                copy.start()

        @pl.when(last)
        def _():
            for copy in chunk_sends(e_low_in, 1):
                copy.start()

        @pl.when(jnp.logical_not(first))
        def _():
            first_sends[0].start()

        @pl.when(jnp.logical_not(last))
        def _():
            first_sends[1].start()
    else:
        first_sends[0].start()
        first_sends[1].start()
    first_sends[2].start()
    first_sends[3].start()
    if spread:
        @pl.when(helper & (half == 1))
        def _():
            forward()

    double_layer(ket_ref, gate_ref, quench_ref, gx * nrow + gy, mirror, w_ref)
    for copy in local:
        copy.wait()
    for cut in (0, 1):
        transposed_edge(own.at[cut], et_own.at[cut])

    def interleave(turned):
        for l in range(B):
            value = jnp.concatenate(
                [west_nat[:, l * CHI : (l + 1) * CHI].astype(F32), jnp.zeros((CHI, L - CHI), F32)], axis=1
            )
            if turned:
                value = jnp.concatenate([value, jnp.zeros((L - CHI, L), F32)], axis=0).T[0:CHI, :]
            inter[pl.ds(l, CHI, stride=B), :] = value

    @pl.when(mirror)
    def _():
        interleave(True)

    @pl.when(jnp.logical_not(mirror))
    def _():
        interleave(False)

    west[...] = inter[...].astype(BF)

    def arrive(cut):
        remote(near.at[cut], near.at[cut], cut, north).wait_recv()
        remote(c_in.at[0], c_in.at[0], 2 + cut, north).wait_recv()
        for i in (2 * cut, 2 * cut + 1):
            cpad[i] = jnp.zeros((L, L), BF)
            cpad[i, 0:CHI, :] = jnp.concatenate([c_in[i], jnp.zeros((CHI, L - CHI), BF)], axis=1)
        transposed_edge(near.at[cut], et_near.at[cut])

    def corner_send(cut):
        pair = pl.ds(2 * cut, 2)
        return remote(c_send.at[pair], c_recv.at[pair], 4 + cut, east)

    last_corners = [
        remote(c_fin.at[flip], c_low_out.at[0, 0], 7, east),
        remote(c_fin.at[1 - flip], c_up_out.at[0, 0], 8, east),
    ]

    def chain(step, cut):
        if step == 0:
            arrive(cut)
        else:
            corner_send(cut).wait_recv()
        corners = cpad if step == 0 else c_recv
        for piece in range(8):
            rows = slice(piece * 256, (piece + 1) * 256)
            mine = nt(et_own[cut, rows, :], corners[2 * cut])
            other = nt(et_near[cut, rows, :], corners[2 * cut + 1])
            for i, value in enumerate(((mine + other), mine, other)):
                value = value.astype(BF)
                for side in range(2):
                    at = piece * 256 + side * L
                    glu[i * L : (i + 1) * L, at : at + L] = value[side * L : (side + 1) * L, :]
        sums = nt(glu[0:L, :], glu[...])
        if cut == 1:
            for d in range(B):
                rows = slice(d * L, (d + 1) * L)
                value = nt(corners[2], et_own[1, rows, :]) + nt(corners[3], et_near[1, rows, :])
                inter[pl.ds(d, CHI, stride=B), :] = value[0:CHI, :]
        m = polar_right(sums[:, 0:L])
        new_own = unit_corner(product(m, sums[:, L : 2 * L]))
        if step < STEPS - 1:
            c_send[2 * cut] = new_own
            c_send[2 * cut + 1] = unit_corner(product(m, sums[:, 2 * L : 3 * L]))
            corner_send(cut).start()
        else:
            c_fin[cut] = new_own[0:CHI, 0:CHI]
        m_rows = jnp.concatenate(list(split(m)), axis=0)
        if cut == 0:
            for piece in range(8):
                both = nn(m_rows, glu[0:L, piece * 256 : (piece + 1) * 256])
                both = (both[0:L] + both[L : 2 * L]).astype(BF)
                for side in range(2):
                    at = piece * 256 + side * L
                    pt[at : at + L, :] = both[:, side * L : (side + 1) * L]
        else:
            for piece in range(6):
                rows = slice(piece * 256, (piece + 1) * 256)
                both = nt(m_rows, inter[rows, :].astype(BF))
                pup[:, rows] = (both[0:CHI] + both[L : L + CHI]).astype(BF)

    def contract(left):
        def spread_rows(k):
            rows = left[k * 256 : (k + 1) * 256, :]
            for pair in range(8):
                out = nt(rows, pt[pair * 256 : (pair + 1) * 256, :]).astype(BF)
                fs[k, 2 * pair] = out[:, 0:L]
                fs[k, 2 * pair + 1] = out[:, L : 2 * L]

        def absorb(k):
            for pair in range(8):
                cols = [
                    jnp.concatenate([fs[k, d, u * B : (u + 1) * B, :] for d in range(B)], axis=0)
                    for u in (2 * pair, 2 * pair + 1)
                ]
                out = nn(w_ref[...], jnp.concatenate(cols, axis=1)).astype(BF)
                for side in range(2):
                    at = k * 256 + (2 * pair + side) * B
                    for r in range(B):
                        t_ref[r // 2, at : at + B, (r % 2) * L : (r % 2 + 1) * L] = out[
                            r * B : (r + 1) * B, side * L : (side + 1) * L
                        ]

        spread_rows(0)
        for k in range(6):
            if k < 5:
                spread_rows(k + 1)
            absorb(k)

    def close(store):
        square = jnp.zeros((CHI, CHI), F32)
        for pair in range(8):
            out = nn(pup[...], t_ref[pair])
            for side in range(2):
                value = out[:, side * L : side * L + CHI]
                square = square + value * value
                store(2 * pair + side, jnp.concatenate([value, jnp.zeros((CHI, L - CHI), F32)], axis=1))
        return lax.rsqrt(jnp.sum(square) * (1.0 / (CHI * CHI * B)) + 1e-06)

    chain(0, 0)
    contract(west)
    chain(1, 0)
    if spread:
        @pl.when(helper & (half == 0))
        def _():
            forward()

    chain(0, 1)

    def store_west(r, value):
        inter[pl.ds(r, CHI, stride=B), :] = value

    scale = close(store_west)
    west_send[...] = (inter[...] * scale).astype(BF)
    west_shift = remote(west_send, west_recv, 6, east)
    west_shift.start()
    chain(1, 1)
    for copy in last_corners:
        copy.start()
    west_shift.wait_recv()
    contract(west_recv)

    def store_last(r, value):
        fin[r, 0:CHI, :] = value

    scale = close(store_last)

    @pl.when(mirror)
    def _():
        e_fin[...] = jnp.concatenate([(fin[r].T[0:CHI, 0:CHI] * scale).astype(BF) for r in range(B)], axis=1)

    @pl.when(jnp.logical_not(mirror))
    def _():
        e_fin[...] = jnp.concatenate([(fin[r, 0:CHI, 0:CHI] * scale).astype(BF) for r in range(B)], axis=1)

    edge_shift = remote(e_fin, e_out.at[0, 0], 9, east)
    edge_shift.start()
    for copy in last_corners + [edge_shift]:
        copy.wait_recv()
    for copy in last_corners + [edge_shift, west_shift, corner_send(0), corner_send(1)] + first_sends[2:]:
        copy.wait_send()
    if spread:
        @pl.when(first)
        def _():
            for copy in chunk_sends(e_up_in, 0):
                copy.wait_send()

        @pl.when(last)
        def _():
            for copy in chunk_sends(e_low_in, 1):
                copy.wait_send()

        @pl.when(jnp.logical_not(first))
        def _():
            first_sends[0].wait_send()

        @pl.when(jnp.logical_not(last))
        def _():
            first_sends[1].wait_send()

        @pl.when(helper)
        def _():
            for copy in forwards():
                copy.wait_send()
    else:
        first_sends[0].wait_send()
        first_sends[1].wait_send()


def per_device(c_upper, edge_upper, edge_left, c_lower, edge_lower, site_ket, time_gate, quench_sites):
    hbm = pl.BlockSpec(memory_space=pl.ANY)
    vmem = pl.BlockSpec(memory_space=pltpu.VMEM)
    smem = pl.BlockSpec(memory_space=pltpu.SMEM)
    corner = jax.ShapeDtypeStruct((1, 1, CHI, CHI), BF)
    edge = jax.ShapeDtypeStruct((1, 1, CHI, B * CHI), BF)
    inner = pltpu.VMEM((CHI * B, L), BF)
    four = pltpu.VMEM((4, L, L), BF)
    two_edges = pltpu.VMEM((2, CHI, B * CHI), BF)
    two_tall = pltpu.VMEM((2, B * L, L), BF)
    dma = pltpu.SemaphoreType.DMA
    return pl.pallas_call(
        kernel,
        out_shape=(corner, edge, corner),
        in_specs=[hbm] * 5 + [vmem, smem, smem],
        out_specs=(hbm,) * 3,
        scratch_shapes=[
            two_edges, two_edges, pltpu.VMEM((CHI, B * CHI), BF), pltpu.VMEM((4, CHI, CHI), BF),
            two_tall, two_tall, four, four, four, pltpu.VMEM((256, 256), BF),
            inner, inner, inner, pltpu.VMEM((3 * L, B * L), BF), pltpu.VMEM((CHI * B, L), F32),
            pltpu.VMEM((CHI, CHI * B), BF), pltpu.VMEM((B * L, L), BF), pltpu.VMEM((6, B, 256, L), BF),
            pltpu.VMEM((8, CHI * B, 2 * L), BF), pltpu.VMEM((B, L, L), F32),
            pltpu.VMEM((CHI, B * CHI), BF), pltpu.VMEM((2, CHI, CHI), BF),
            pltpu.VMEM((2, CHI, L), BF),
            dma((5,)), dma((10,)), dma((10,)), dma((CHUNKS,)), dma((2,)),
        ],
        compiler_params=pltpu.CompilerParams(
            collective_id=0, has_side_effects=True, vmem_limit_bytes=63 * 1024 * 1024
        ),
        name="left_move",
    )(c_upper, edge_upper, edge_left, c_lower, edge_lower, site_ket, time_gate, quench_sites)


def solution(mesh):
    site = P("gx", "gy", None, None)
    return jax.shard_map(
        per_device,
        mesh=mesh,
        in_specs=(site,) * 6 + (P(), P()),
        out_specs=(site,) * 3,
        check_vma=False,
    )
```

```python
import jax
import jax.numpy as jnp
from jax import lax
from jax.experimental import pallas as pl
from jax.experimental.pallas import tpu as pltpu
from jax.sharding import PartitionSpec as P

NS_ITERS = 6
STEPS = 2
MESH = pl.DeviceIdType.MESH
CHI = 96
B = 16
HALF = 16
CHUNKS = 12
L = 128
F32 = jnp.float32
BF = jnp.bfloat16


def nt(a, b):
    return lax.dot_general(a, b, (((1,), (1,)), ((), ())), preferred_element_type=F32)


def nn(a, b):
    return jnp.dot(a, b, preferred_element_type=F32)


def split(x):
    hi = x.astype(BF)
    return hi, (x - hi.astype(F32)).astype(BF)


def product(a, b):
    a_hi, a_lo = split(a)
    b_hi, b_lo = split(b)
    return nn(
        jnp.concatenate([a_hi, a_lo], axis=1), jnp.concatenate([b_hi, b_hi], axis=0)
    ) + nn(a_hi, b_lo)


def eye():
    row = lax.broadcasted_iota(jnp.int32, (L, L), 0)
    col = lax.broadcasted_iota(jnp.int32, (L, L), 1)
    return jnp.where((row == col) & (row < CHI), 1.0, 0.0).astype(F32)


def polar_right(gram):
    one = eye()
    scale = 1.0 / (jnp.sum(gram * one) + 1e-06)
    s = gram * scale
    p = 1.5 * one - 0.5 * s
    m = p
    for _ in range(NS_ITERS - 1):
        s = product(product(s, p), p)
        p = 1.5 * one - 0.5 * s
        m = product(m, p)
    return m * jnp.sqrt(scale)


def unit_corner(x):
    return (x * lax.rsqrt(jnp.sum(x * x) * (1.0 / (CHI * CHI)) + 1e-06)).astype(BF)


def transposed_edge(edge_ref, out_ref):
    for chunk in range(4):
        lanes = edge_ref[:, chunk * 384 : (chunk + 1) * 384]
        lanes = jnp.concatenate([lanes, jnp.zeros((L - CHI, 384), BF)], axis=0)
        turned = lanes.T
        for i in range(4):
            d = chunk * 4 + i
            out_ref[d * L : d * L + CHI, :] = turned[i * CHI : (i + 1) * CHI, :]
            out_ref[d * L + CHI : (d + 1) * L, :] = jnp.zeros((L - CHI, L), BF)


def double_layer(ket_ref, gate_ref, quench_ref, own_index, mirror, out_ref):
    n = lax.broadcasted_iota(jnp.int32, (256, 256), 0)
    m = lax.broadcasted_iota(jnp.int32, (256, 256), 1)
    f4 = lambda x, k: (x >> (6 - 2 * k)) & 3
    outer = jnp.where(mirror, f4(m, 3), f4(m, 1))
    inner = jnp.where(mirror, f4(n, 1), f4(n, 3))
    ket_mask = (f4(n, 2) == outer) & (f4(n, 0) == f4(m, 2))
    bra_mask = (f4(n, 3) == outer) & (f4(n, 1) == f4(m, 2))
    ket_spread = ((f4(n, 0) == f4(m, 2)) & (inner == f4(m, 0))).astype(F32).astype(BF)
    bra_spread = ((f4(n, 0) == f4(m, 3)) & (inner == f4(m, 1))).astype(F32).astype(BF)
    chosen = quench_ref[0] == own_index
    for i in range(1, 4):
        chosen = chosen | (quench_ref[i] == own_index)
    kets = [ket_ref[0, 0, s : s + 1, :].astype(F32) for s in range(2)]
    total = jnp.zeros((256, 256), F32)
    for s in range(2):
        bra = jnp.zeros((1, 256), F32)
        for t in range(2):
            gram = gate_ref[0, s] * gate_ref[0, t] + gate_ref[1, s] * gate_ref[1, t]
            weight = jnp.where(chosen, gram, 1.0 if s == t else 0.0)
            bra = bra + weight * kets[t]
        bra = bra.astype(BF).astype(F32)
        ket_part = nn(jnp.where(ket_mask, kets[s], 0.0).astype(BF), ket_spread)
        bra_part = nn(jnp.where(bra_mask, bra, 0.0).astype(BF), bra_spread)
        total = total + ket_part * bra_part
    out_ref[...] = total.astype(BF)


def kernel(
    c_up_in, e_up_in, e_left_in, c_low_in, e_low_in, ket_ref, gate_ref, quench_ref,
    c_up_out, e_out, c_low_out,
    own, near, west_nat, c_in, et_own, et_near, cpad, c_send, c_recv, w_ref,
    west, west_recv, west_send, glu, inter, pup, pt, fs, t_ref, fin, e_fin, c_fin,
    hop, lsem, ssem, rsem, psem, hsem, ready,
):
    gx, gy = lax.axis_index("gx"), lax.axis_index("gy")
    ncol, nrow = lax.axis_size("gx"), lax.axis_size("gy")
    north = (gx, lax.rem(gy + nrow - 1, nrow))
    south = (gx, lax.rem(gy + 1, nrow))
    east = (lax.rem(gx + 1, ncol), gy)
    before = (lax.rem(gx + ncol - 1, ncol), gy)
    spread = nrow == 2 * HALF
    period = HALF if spread else nrow
    half, place = gy // period, lax.rem(gy, period)
    first, last = place == 0, place == period - 1
    helper = (place >= 2) & (place < 2 + CHUNKS)
    mirror = last
    flip = jnp.where(mirror, 1, 0)
    barrier = pltpu.get_barrier_semaphore()

    def greet(peer):
        pl.semaphore_signal(barrier, inc=1, device_id=peer, device_id_type=MESH)

    edge_row = first | last
    far = jnp.where(first, (1 - half) * HALF + HALF - 1, (1 - half) * HALF)
    greet(before)
    if spread:
        @pl.when(jnp.logical_not(first & (half == 1)))
        def _():
            greet(north)

        @pl.when(jnp.logical_not(last & (half == 1)))
        def _():
            greet(south)

        @pl.when(edge_row & (half == 0))
        def _():
            for c in range(CHUNKS):
                greet((gx, HALF + 2 + c))

        @pl.when(helper)
        def _():
            greet((gx, half * HALF))
            greet((gx, half * HALF + HALF - 1))

        @pl.when(helper & (half == 0))
        def _():
            greet((gx, HALF))
            greet((gx, 2 * HALF - 1))

        greeted = (
            3
            + jnp.where(helper & (half == 1), 2, 0)
            + jnp.where(edge_row, CHUNKS, 0)
            + jnp.where(edge_row & (half == 1), CHUNKS, 0)
            - jnp.where(edge_row & (half == 0), 1, 0)
        )
    else:
        greet(north)
        greet(south)
        greeted = 3

    local = [
        pltpu.make_async_copy(src.at[0, 0], dst, lsem.at[i])
        for i, (src, dst) in enumerate((
            (e_low_in, own.at[flip]), (e_up_in, own.at[1 - flip]), (e_left_in, west_nat),
            (c_low_in, c_in.at[2 * flip]), (c_up_in, c_in.at[2 - 2 * flip]),
        ))
    ]
    for copy in local:
        copy.start()
    pl.semaphore_wait(barrier, greeted)
    if spread:
        @pl.when(edge_row & (half == 1))
        def _():
            for row in [far] + [2 + c for c in range(CHUNKS)]:
                pl.semaphore_signal(ready, inc=1, device_id=(gx, row), device_id_type=MESH)


    def remote(src, dst, i, peer, j=None):
        return pltpu.make_async_remote_copy(
            src_ref=src, dst_ref=dst, send_sem=ssem.at[i], recv_sem=rsem.at[i if j is None else j],
            device_id=peer, device_id_type=MESH,
        )

    to_north = jnp.where(first, 1, 0)
    to_south = jnp.where(place == period - 2, 0, 1)
    first_sends = [
        remote(e_up_in.at[0, 0], near.at[to_north], 0, north, to_north),
        remote(e_low_in.at[0, 0], near.at[to_south], 1, south, to_south),
        remote(c_up_in.at[0, 0], c_in.at[1 + 2 * to_north], 2, north, 2 + to_north),
        remote(c_low_in.at[0, 0], c_in.at[1 + 2 * to_south], 3, south, 2 + to_south),
    ]

    def relay(src, dst, send, recv, peer):
        return pltpu.make_async_remote_copy(
            src_ref=src, dst_ref=dst, send_sem=psem.at[send], recv_sem=recv,
            device_id=peer, device_id_type=MESH,
        )

    def chunk_sends(edge_in, slot):
        return [
            relay(edge_in.at[0, 0, :, pl.ds(c * L, L)], hop.at[slot], c, hsem.at[slot], (gx, half * HALF + 2 + c))
            for c in range(CHUNKS)
        ]

    lanes = pl.ds(pl.multiple_of((place - 2) * L, L), L)

    def forwards():
        return [
            relay(hop.at[0], near.at[1, :, lanes], 0, rsem.at[1], (gx, (1 - half) * HALF + HALF - 1)),
            relay(hop.at[1], near.at[1, :, lanes], 1, rsem.at[1], (gx, (1 - half) * HALF)),
        ]

    def forward():
        @pl.when(half == 0)
        def _():
            pl.semaphore_wait(ready, 2)

        for slot, copy in enumerate(forwards()):
            relay(hop.at[slot], hop.at[slot], slot, hsem.at[slot], north).wait_recv()
            copy.start()

    if spread:
        @pl.when(first)
        def _():
            for copy in chunk_sends(e_up_in, 0):
                copy.start()

        @pl.when(last)
        def _():
            for copy in chunk_sends(e_low_in, 1):
                copy.start()

        @pl.when(jnp.logical_not(first))
        def _():
            first_sends[0].start()

        @pl.when(jnp.logical_not(last))
        def _():
            first_sends[1].start()
    else:
        first_sends[0].start()
        first_sends[1].start()
        first_sends[2].start()
        first_sends[3].start()
    if spread:
        @pl.when(jnp.logical_not(first & (half == 0)))
        def _():
            first_sends[2].start()

        @pl.when(jnp.logical_not(last & (half == 0)))
        def _():
            first_sends[3].start()

        @pl.when(helper & (half == 1))
        def _():
            forward()

    double_layer(ket_ref, gate_ref, quench_ref, gx * nrow + gy, mirror, w_ref)
    for copy in local:
        copy.wait()
    for cut in (0, 1):
        transposed_edge(own.at[cut], et_own.at[cut])

    def interleave(turned):
        for l in range(B):
            value = jnp.concatenate(
                [west_nat[:, l * CHI : (l + 1) * CHI].astype(F32), jnp.zeros((CHI, L - CHI), F32)], axis=1
            )
            if turned:
                value = jnp.concatenate([value, jnp.zeros((L - CHI, L), F32)], axis=0).T[0:CHI, :]
            inter[pl.ds(l, CHI, stride=B), :] = value

    @pl.when(mirror)
    def _():
        interleave(True)

    @pl.when(jnp.logical_not(mirror))
    def _():
        interleave(False)

    west[...] = inter[...].astype(BF)

    def arrive(cut):
        remote(near.at[cut], near.at[cut], cut, north).wait_recv()
        remote(c_in.at[0], c_in.at[0], 2 + cut, north).wait_recv()
        for i in (2 * cut, 2 * cut + 1):
            cpad[i] = jnp.zeros((L, L), BF)
            cpad[i, 0:CHI, :] = jnp.concatenate([c_in[i], jnp.zeros((CHI, L - CHI), BF)], axis=1)
        transposed_edge(near.at[cut], et_near.at[cut])

    def corner_send(cut):
        pair = pl.ds(2 * cut, 2)
        return remote(c_send.at[pair], c_recv.at[pair], 4 + cut, east)

    last_corners = [
        remote(c_fin.at[flip], c_low_out.at[0, 0], 7, east),
        remote(c_fin.at[1 - flip], c_up_out.at[0, 0], 8, east),
    ]

    def chain(step, cut):
        if step == 0:
            arrive(cut)
        else:
            corner_send(cut).wait_recv()
        corners = cpad if step == 0 else c_recv
        for piece in range(8):
            rows = slice(piece * 256, (piece + 1) * 256)
            mine = nt(et_own[cut, rows, :], corners[2 * cut])
            other = nt(et_near[cut, rows, :], corners[2 * cut + 1])
            for i, value in enumerate(((mine + other), mine, other)):
                value = value.astype(BF)
                for side in range(2):
                    at = piece * 256 + side * L
                    glu[i * L : (i + 1) * L, at : at + L] = value[side * L : (side + 1) * L, :]
        sums = nt(glu[0:L, :], glu[...])
        if cut == 1:
            for d in range(B):
                rows = slice(d * L, (d + 1) * L)
                value = nt(corners[2], et_own[1, rows, :]) + nt(corners[3], et_near[1, rows, :])
                inter[pl.ds(d, CHI, stride=B), :] = value[0:CHI, :]
        m = polar_right(sums[:, 0:L])
        new_own = unit_corner(product(m, sums[:, L : 2 * L]))
        if step < STEPS - 1:
            c_send[2 * cut] = new_own
            c_send[2 * cut + 1] = unit_corner(product(m, sums[:, 2 * L : 3 * L]))
            corner_send(cut).start()
        else:
            c_fin[cut] = new_own[0:CHI, 0:CHI]
        m_rows = jnp.concatenate(list(split(m)), axis=0)
        if cut == 0:
            for piece in range(8):
                both = nn(m_rows, glu[0:L, piece * 256 : (piece + 1) * 256])
                both = (both[0:L] + both[L : 2 * L]).astype(BF)
                for side in range(2):
                    at = piece * 256 + side * L
                    pt[at : at + L, :] = both[:, side * L : (side + 1) * L]
        else:
            for piece in range(6):
                rows = slice(piece * 256, (piece + 1) * 256)
                both = nt(m_rows, inter[rows, :].astype(BF))
                pup[:, rows] = (both[0:CHI] + both[L : L + CHI]).astype(BF)

    def contract(left):
        def spread_rows(k):
            rows = left[k * 256 : (k + 1) * 256, :]
            for pair in range(8):
                out = nt(rows, pt[pair * 256 : (pair + 1) * 256, :]).astype(BF)
                fs[k, 2 * pair] = out[:, 0:L]
                fs[k, 2 * pair + 1] = out[:, L : 2 * L]

        def absorb(k):
            for pair in range(8):
                cols = [
                    jnp.concatenate([fs[k, d, u * B : (u + 1) * B, :] for d in range(B)], axis=0)
                    for u in (2 * pair, 2 * pair + 1)
                ]
                out = nn(w_ref[...], jnp.concatenate(cols, axis=1)).astype(BF)
                for side in range(2):
                    at = k * 256 + (2 * pair + side) * B
                    for r in range(B):
                        t_ref[r // 2, at : at + B, (r % 2) * L : (r % 2 + 1) * L] = out[
                            r * B : (r + 1) * B, side * L : (side + 1) * L
                        ]

        spread_rows(0)
        for k in range(6):
            if k < 5:
                spread_rows(k + 1)
            absorb(k)

    def close(store):
        square = jnp.zeros((CHI, CHI), F32)
        for pair in range(8):
            out = nn(pup[...], t_ref[pair])
            for side in range(2):
                value = out[:, side * L : side * L + CHI]
                square = square + value * value
                store(2 * pair + side, jnp.concatenate([value, jnp.zeros((CHI, L - CHI), F32)], axis=1))
        return lax.rsqrt(jnp.sum(square) * (1.0 / (CHI * CHI * B)) + 1e-06)

    chain(0, 0)
    contract(west)
    chain(1, 0)
    if spread:
        @pl.when(first & (half == 0))
        def _():
            pl.semaphore_wait(ready, 1)
            first_sends[2].start()

        @pl.when(last & (half == 0))
        def _():
            pl.semaphore_wait(ready, 1)
            first_sends[3].start()

        @pl.when(helper & (half == 0))
        def _():
            forward()

    chain(0, 1)

    def store_west(r, value):
        inter[pl.ds(r, CHI, stride=B), :] = value

    scale = close(store_west)
    west_send[...] = (inter[...] * scale).astype(BF)
    west_shift = remote(west_send, west_recv, 6, east)
    west_shift.start()
    chain(1, 1)
    for copy in last_corners:
        copy.start()
    west_shift.wait_recv()
    contract(west_recv)

    def store_last(r, value):
        fin[r, 0:CHI, :] = value

    scale = close(store_last)

    @pl.when(mirror)
    def _():
        e_fin[...] = jnp.concatenate([(fin[r].T[0:CHI, 0:CHI] * scale).astype(BF) for r in range(B)], axis=1)

    @pl.when(jnp.logical_not(mirror))
    def _():
        e_fin[...] = jnp.concatenate([(fin[r, 0:CHI, 0:CHI] * scale).astype(BF) for r in range(B)], axis=1)

    edge_shift = remote(e_fin, e_out.at[0, 0], 9, east)
    edge_shift.start()
    for copy in last_corners + [edge_shift]:
        copy.wait_recv()
    for copy in last_corners + [edge_shift, west_shift, corner_send(0), corner_send(1)] + first_sends[2:]:
        copy.wait_send()
    if spread:
        @pl.when(first)
        def _():
            for copy in chunk_sends(e_up_in, 0):
                copy.wait_send()

        @pl.when(last)
        def _():
            for copy in chunk_sends(e_low_in, 1):
                copy.wait_send()

        @pl.when(jnp.logical_not(first))
        def _():
            first_sends[0].wait_send()

        @pl.when(jnp.logical_not(last))
        def _():
            first_sends[1].wait_send()

        @pl.when(helper)
        def _():
            for copy in forwards():
                copy.wait_send()
    else:
        first_sends[0].wait_send()
        first_sends[1].wait_send()


def settle(*refs):
    sources, targets, stages, sem = refs[0:3], refs[3:6], refs[6:9], refs[9]
    fetch = [pltpu.make_async_copy(sources[i], stages[i], sem.at[i]) for i in range(3)]
    keep = [pltpu.make_async_copy(stages[i], targets[i], sem.at[3 + i]) for i in range(3)]
    for copy in fetch:
        copy.start()
    for i in (0, 2, 1):
        fetch[i].wait()
        keep[i].start()
    for copy in keep:
        copy.wait()


def per_device(c_upper, edge_upper, edge_left, c_lower, edge_lower, site_ket, time_gate, quench_sites):
    hbm = pl.BlockSpec(memory_space=pl.ANY)
    vmem = pl.BlockSpec(memory_space=pltpu.VMEM)
    smem = pl.BlockSpec(memory_space=pltpu.SMEM)
    corner = jax.ShapeDtypeStruct((1, 1, CHI, CHI), BF)
    edge = jax.ShapeDtypeStruct((1, 1, CHI, B * CHI), BF)
    inner = pltpu.VMEM((CHI * B, L), BF)
    four = pltpu.VMEM((4, L, L), BF)
    two_edges = pltpu.VMEM((2, CHI, B * CHI), BF)
    two_tall = pltpu.VMEM((2, B * L, L), BF)
    dma = pltpu.SemaphoreType.DMA
    moved = pl.pallas_call(
        kernel,
        out_shape=(corner, edge, corner),
        in_specs=[hbm] * 5 + [vmem, smem, smem],
        out_specs=(hbm,) * 3,
        scratch_shapes=[
            two_edges, two_edges, pltpu.VMEM((CHI, B * CHI), BF), pltpu.VMEM((4, CHI, CHI), BF),
            two_tall, two_tall, four, four, four, pltpu.VMEM((256, 256), BF),
            inner, inner, inner, pltpu.VMEM((3 * L, B * L), BF), pltpu.VMEM((CHI * B, L), F32),
            pltpu.VMEM((CHI, CHI * B), BF), pltpu.VMEM((B * L, L), BF), pltpu.VMEM((6, B, 256, L), BF),
            pltpu.VMEM((8, CHI * B, 2 * L), BF), pltpu.VMEM((B, L, L), F32),
            pltpu.VMEM((CHI, B * CHI), BF), pltpu.VMEM((2, CHI, CHI), BF),
            pltpu.VMEM((2, CHI, L), BF),
            dma((5,)), dma((10,)), dma((10,)), dma((CHUNKS,)), dma((2,)),
            pltpu.SemaphoreType.REGULAR,
        ],
        compiler_params=pltpu.CompilerParams(
            collective_id=0, has_side_effects=True, vmem_limit_bytes=63 * 1024 * 1024
        ),
        name="left_move",
    )(c_upper, edge_upper, edge_left, c_lower, edge_lower, site_ket, time_gate, quench_sites)
    return pl.pallas_call(
        settle,
        out_shape=(corner, edge, corner),
        in_specs=[hbm] * 3,
        out_specs=(hbm,) * 3,
        scratch_shapes=[
            pltpu.VMEM((1, 1, CHI, CHI), BF), pltpu.VMEM((1, 1, CHI, B * CHI), BF), pltpu.VMEM((1, 1, CHI, CHI), BF),
            pltpu.SemaphoreType.DMA((6,)),
        ],
        compiler_params=pltpu.CompilerParams(vmem_limit_bytes=63 * 1024 * 1024),
        name="settle",
    )(*moved)


def solution(mesh):
    site = P("gx", "gy", None, None)
    return jax.shard_map(
        per_device,
        mesh=mesh,
        in_specs=(site,) * 6 + (P(), P()),
        out_specs=(site,) * 3,
        check_vma=False,
    )
```

```python
import jax
import jax.numpy as jnp
from jax import lax
from jax.experimental import pallas as pl
from jax.experimental.pallas import tpu as pltpu
from jax.sharding import PartitionSpec as P

NS_ITERS = 6
STEPS = 2
MESH = pl.DeviceIdType.MESH
CHI = 96
B = 16
HALF = 16
CHUNKS = 12
L = 128
F32 = jnp.float32
BF = jnp.bfloat16


def nt(a, b):
    return lax.dot_general(a, b, (((1,), (1,)), ((), ())), preferred_element_type=F32)


def nn(a, b):
    return jnp.dot(a, b, preferred_element_type=F32)


def split(x):
    hi = x.astype(BF)
    return hi, (x - hi.astype(F32)).astype(BF)


def product(a, b):
    a_hi, a_lo = split(a)
    b_hi, b_lo = split(b)
    return nn(
        jnp.concatenate([a_hi, a_lo], axis=1), jnp.concatenate([b_hi, b_hi], axis=0)
    ) + nn(a_hi, b_lo)


def eye():
    row = lax.broadcasted_iota(jnp.int32, (L, L), 0)
    col = lax.broadcasted_iota(jnp.int32, (L, L), 1)
    return jnp.where((row == col) & (row < CHI), 1.0, 0.0).astype(F32)


def polar_right(gram):
    one = eye()
    scale = 1.0 / (jnp.sum(gram * one) + 1e-06)
    s = gram * scale
    p = 1.5 * one - 0.5 * s
    m = p
    for _ in range(NS_ITERS - 1):
        s = product(product(s, p), p)
        p = 1.5 * one - 0.5 * s
        m = product(m, p)
    return m * jnp.sqrt(scale)


def unit_corner(x):
    return (x * lax.rsqrt(jnp.sum(x * x) * (1.0 / (CHI * CHI)) + 1e-06)).astype(BF)


def transposed_edge(edge_ref, out_ref):
    for chunk in range(4):
        lanes = edge_ref[:, chunk * 384 : (chunk + 1) * 384]
        lanes = jnp.concatenate([lanes, jnp.zeros((L - CHI, 384), BF)], axis=0)
        turned = lanes.T
        for i in range(4):
            d = chunk * 4 + i
            out_ref[d * L : d * L + CHI, :] = turned[i * CHI : (i + 1) * CHI, :]
            out_ref[d * L + CHI : (d + 1) * L, :] = jnp.zeros((L - CHI, L), BF)


def double_layer(ket_ref, gate_ref, quench_ref, own_index, mirror, out_ref):
    n = lax.broadcasted_iota(jnp.int32, (256, 256), 0)
    m = lax.broadcasted_iota(jnp.int32, (256, 256), 1)
    f4 = lambda x, k: (x >> (6 - 2 * k)) & 3
    outer = jnp.where(mirror, f4(m, 3), f4(m, 1))
    inner = jnp.where(mirror, f4(n, 1), f4(n, 3))
    ket_mask = (f4(n, 2) == outer) & (f4(n, 0) == f4(m, 2))
    bra_mask = (f4(n, 3) == outer) & (f4(n, 1) == f4(m, 2))
    ket_spread = ((f4(n, 0) == f4(m, 2)) & (inner == f4(m, 0))).astype(F32).astype(BF)
    bra_spread = ((f4(n, 0) == f4(m, 3)) & (inner == f4(m, 1))).astype(F32).astype(BF)
    chosen = quench_ref[0] == own_index
    for i in range(1, 4):
        chosen = chosen | (quench_ref[i] == own_index)
    kets = [ket_ref[0, 0, s : s + 1, :].astype(F32) for s in range(2)]
    total = jnp.zeros((256, 256), F32)
    for s in range(2):
        bra = jnp.zeros((1, 256), F32)
        for t in range(2):
            gram = gate_ref[0, s] * gate_ref[0, t] + gate_ref[1, s] * gate_ref[1, t]
            weight = jnp.where(chosen, gram, 1.0 if s == t else 0.0)
            bra = bra + weight * kets[t]
        bra = bra.astype(BF).astype(F32)
        ket_part = nn(jnp.where(ket_mask, kets[s], 0.0).astype(BF), ket_spread)
        bra_part = nn(jnp.where(bra_mask, bra, 0.0).astype(BF), bra_spread)
        total = total + ket_part * bra_part
    out_ref[...] = total.astype(BF)


def kernel(
    c_up_in, e_up_in, e_left_in, c_low_in, e_low_in, ket_ref, gate_ref, quench_ref,
    c_up_out, e_out, c_low_out,
    own, near, west_nat, c_in, et_own, et_near, cpad, c_send, c_recv, w_ref,
    west, west_recv, west_send, glu, inter, pup, pt, fs, t_ref, fin, e_fin, c_fin,
    hop, lsem, ssem, rsem, psem, hsem, wsend, wrecv, ready,
):
    gx, gy = lax.axis_index("gx"), lax.axis_index("gy")
    ncol, nrow = lax.axis_size("gx"), lax.axis_size("gy")
    north = (gx, lax.rem(gy + nrow - 1, nrow))
    south = (gx, lax.rem(gy + 1, nrow))
    east = (lax.rem(gx + 1, ncol), gy)
    before = (lax.rem(gx + ncol - 1, ncol), gy)
    spread = nrow == 2 * HALF
    period = HALF if spread else nrow
    half, place = gy // period, lax.rem(gy, period)
    first, last = place == 0, place == period - 1
    helper = (place >= 2) & (place < 2 + CHUNKS)
    mirror = last
    flip = jnp.where(mirror, 1, 0)
    barrier = pltpu.get_barrier_semaphore()

    def greet(peer):
        pl.semaphore_signal(barrier, inc=1, device_id=peer, device_id_type=MESH)

    edge_row = first | last
    far = jnp.where(first, (1 - half) * HALF + HALF - 1, (1 - half) * HALF)
    greet(before)
    if spread:
        @pl.when(jnp.logical_not(first & (half == 1)))
        def _():
            greet(north)

        @pl.when(jnp.logical_not(last & (half == 1)))
        def _():
            greet(south)

        @pl.when(edge_row & (half == 0))
        def _():
            for c in range(CHUNKS):
                greet((gx, HALF + 2 + c))

        @pl.when(helper)
        def _():
            greet((gx, half * HALF))
            greet((gx, half * HALF + HALF - 1))

        @pl.when(helper & (half == 0))
        def _():
            greet((gx, HALF))
            greet((gx, 2 * HALF - 1))

        greeted = (
            3
            + jnp.where(helper & (half == 1), 2, 0)
            + jnp.where(edge_row, CHUNKS, 0)
            + jnp.where(edge_row & (half == 1), CHUNKS, 0)
            - jnp.where(edge_row & (half == 0), 1, 0)
        )
    else:
        greet(north)
        greet(south)
        greeted = 3

    local = [
        pltpu.make_async_copy(src.at[0, 0], dst, lsem.at[i])
        for i, (src, dst) in enumerate((
            (e_low_in, own.at[flip]), (e_up_in, own.at[1 - flip]), (e_left_in, west_nat),
            (c_low_in, c_in.at[2 * flip]), (c_up_in, c_in.at[2 - 2 * flip]),
        ))
    ]
    for copy in local:
        copy.start()
    pl.semaphore_wait(barrier, greeted)
    if spread:
        @pl.when(edge_row & (half == 1))
        def _():
            for row in [far] + [2 + c for c in range(CHUNKS)]:
                pl.semaphore_signal(ready, inc=1, device_id=(gx, row), device_id_type=MESH)


    def remote(src, dst, i, peer, j=None):
        return pltpu.make_async_remote_copy(
            src_ref=src, dst_ref=dst, send_sem=ssem.at[i], recv_sem=rsem.at[i if j is None else j],
            device_id=peer, device_id_type=MESH,
        )

    to_north = jnp.where(first, 1, 0)
    to_south = jnp.where(place == period - 2, 0, 1)
    first_sends = [
        remote(e_up_in.at[0, 0], near.at[to_north], 0, north, to_north),
        remote(e_low_in.at[0, 0], near.at[to_south], 1, south, to_south),
        remote(c_up_in.at[0, 0], c_in.at[1 + 2 * to_north], 2, north, 2 + to_north),
        remote(c_low_in.at[0, 0], c_in.at[1 + 2 * to_south], 3, south, 2 + to_south),
    ]

    def relay(src, dst, send, recv, peer):
        return pltpu.make_async_remote_copy(
            src_ref=src, dst_ref=dst, send_sem=psem.at[send], recv_sem=recv,
            device_id=peer, device_id_type=MESH,
        )

    def chunk_sends(edge_in, slot):
        return [
            relay(edge_in.at[0, 0, :, pl.ds(c * L, L)], hop.at[slot], c, hsem.at[slot], (gx, half * HALF + 2 + c))
            for c in range(CHUNKS)
        ]

    lanes = pl.ds(pl.multiple_of((place - 2) * L, L), L)

    def forwards():
        return [
            relay(hop.at[0], near.at[1, :, lanes], 0, rsem.at[1], (gx, (1 - half) * HALF + HALF - 1)),
            relay(hop.at[1], near.at[1, :, lanes], 1, rsem.at[1], (gx, (1 - half) * HALF)),
        ]

    def forward():
        @pl.when(half == 0)
        def _():
            pl.semaphore_wait(ready, 2)

        for slot, copy in enumerate(forwards()):
            relay(hop.at[slot], hop.at[slot], slot, hsem.at[slot], north).wait_recv()
            copy.start()

    if spread:
        @pl.when(jnp.logical_not(first & (half == 0)))
        def _():
            first_sends[2].start()

        @pl.when(jnp.logical_not(last & (half == 0)))
        def _():
            first_sends[3].start()

        @pl.when(first)
        def _():
            copies = chunk_sends(e_up_in, 0)
            for copy in copies:
                copy.start()
            for copy in copies:
                copy.wait_send()

        @pl.when(last)
        def _():
            copies = chunk_sends(e_low_in, 1)
            for copy in copies:
                copy.start()
            for copy in copies:
                copy.wait_send()

        @pl.when(helper & (half == 1))
        def _():
            forward()

        @pl.when(jnp.logical_not(first))
        def _():
            first_sends[0].start()

        @pl.when(jnp.logical_not(last))
        def _():
            first_sends[1].start()
    else:
        for copy in first_sends:
            copy.start()

    double_layer(ket_ref, gate_ref, quench_ref, gx * nrow + gy, mirror, w_ref)
    for copy in local:
        copy.wait()
    for cut in (0, 1):
        transposed_edge(own.at[cut], et_own.at[cut])

    def interleave(turned):
        for l in range(B):
            value = jnp.concatenate(
                [west_nat[:, l * CHI : (l + 1) * CHI].astype(F32), jnp.zeros((CHI, L - CHI), F32)], axis=1
            )
            if turned:
                value = jnp.concatenate([value, jnp.zeros((L - CHI, L), F32)], axis=0).T[0:CHI, :]
            inter[pl.ds(l, CHI, stride=B), :] = value

    @pl.when(mirror)
    def _():
        interleave(True)

    @pl.when(jnp.logical_not(mirror))
    def _():
        interleave(False)

    west[...] = inter[...].astype(BF)

    def arrive(cut):
        remote(near.at[cut], near.at[cut], cut, north).wait_recv()
        remote(c_in.at[0], c_in.at[0], 2 + cut, north).wait_recv()
        for i in (2 * cut, 2 * cut + 1):
            cpad[i] = jnp.zeros((L, L), BF)
            cpad[i, 0:CHI, :] = jnp.concatenate([c_in[i], jnp.zeros((CHI, L - CHI), BF)], axis=1)
        transposed_edge(near.at[cut], et_near.at[cut])

    def corner_send(cut):
        pair = pl.ds(2 * cut, 2)
        return remote(c_send.at[pair], c_recv.at[pair], 4 + cut, east)

    last_corners = [
        remote(c_fin.at[flip], c_low_out.at[0, 0], 7, east),
        remote(c_fin.at[1 - flip], c_up_out.at[0, 0], 8, east),
    ]

    def chain(step, cut):
        if step == 0:
            arrive(cut)
        else:
            corner_send(cut).wait_recv()
        corners = cpad if step == 0 else c_recv
        for piece in range(8):
            rows = slice(piece * 256, (piece + 1) * 256)
            mine = nt(et_own[cut, rows, :], corners[2 * cut])
            other = nt(et_near[cut, rows, :], corners[2 * cut + 1])
            for i, value in enumerate(((mine + other), mine, other)):
                value = value.astype(BF)
                for side in range(2):
                    at = piece * 256 + side * L
                    glu[i * L : (i + 1) * L, at : at + L] = value[side * L : (side + 1) * L, :]
        sums = nt(glu[0:L, :], glu[...])
        if cut == 1:
            for d in range(B):
                rows = slice(d * L, (d + 1) * L)
                value = nt(corners[2], et_own[1, rows, :]) + nt(corners[3], et_near[1, rows, :])
                inter[pl.ds(d, CHI, stride=B), :] = value[0:CHI, :]
        m = polar_right(sums[:, 0:L])
        new_own = unit_corner(product(m, sums[:, L : 2 * L]))
        if step < STEPS - 1:
            c_send[2 * cut] = new_own
            c_send[2 * cut + 1] = unit_corner(product(m, sums[:, 2 * L : 3 * L]))
            corner_send(cut).start()
        else:
            c_fin[cut] = new_own[0:CHI, 0:CHI]
        m_rows = jnp.concatenate(list(split(m)), axis=0)
        if cut == 0:
            for piece in range(8):
                both = nn(m_rows, glu[0:L, piece * 256 : (piece + 1) * 256])
                both = (both[0:L] + both[L : 2 * L]).astype(BF)
                for side in range(2):
                    at = piece * 256 + side * L
                    pt[at : at + L, :] = both[:, side * L : (side + 1) * L]
        else:
            for piece in range(6):
                rows = slice(piece * 256, (piece + 1) * 256)
                both = nt(m_rows, inter[rows, :].astype(BF))
                pup[:, rows] = (both[0:CHI] + both[L : L + CHI]).astype(BF)

    def contract(left, arrivals=None):
        def spread_rows(k):
            if arrivals is not None and k % 2 == 0:
                arrivals[k // 2].wait_recv()
            rows = left[k * 256 : (k + 1) * 256, :]
            for pair in range(8):
                out = nt(rows, pt[pair * 256 : (pair + 1) * 256, :]).astype(BF)
                fs[k, 2 * pair] = out[:, 0:L]
                fs[k, 2 * pair + 1] = out[:, L : 2 * L]

        def absorb(k):
            for pair in range(8):
                cols = [
                    jnp.concatenate([fs[k, d, u * B : (u + 1) * B, :] for d in range(B)], axis=0)
                    for u in (2 * pair, 2 * pair + 1)
                ]
                out = nn(w_ref[...], jnp.concatenate(cols, axis=1)).astype(BF)
                for side in range(2):
                    at = k * 256 + (2 * pair + side) * B
                    for r in range(B):
                        t_ref[r // 2, at : at + B, (r % 2) * L : (r % 2 + 1) * L] = out[
                            r * B : (r + 1) * B, side * L : (side + 1) * L
                        ]

        spread_rows(0)
        for k in range(6):
            if k < 5:
                spread_rows(k + 1)
            absorb(k)

    def close(store):
        square = jnp.zeros((CHI, CHI), F32)
        for pair in range(8):
            out = nn(pup[...], t_ref[pair])
            for side in range(2):
                value = out[:, side * L : side * L + CHI]
                square = square + value * value
                store(2 * pair + side, jnp.concatenate([value, jnp.zeros((CHI, L - CHI), F32)], axis=1))
        return lax.rsqrt(jnp.sum(square) * (1.0 / (CHI * CHI * B)) + 1e-06)

    chain(0, 0)
    contract(west)
    chain(1, 0)
    if spread:
        @pl.when(first & (half == 0))
        def _():
            pl.semaphore_wait(ready, 1)
            first_sends[2].start()

        @pl.when(last & (half == 0))
        def _():
            pl.semaphore_wait(ready, 1)
            first_sends[3].start()

        @pl.when(helper & (half == 0))
        def _():
            forward()

    chain(0, 1)

    def store_west(r, value):
        inter[pl.ds(r, CHI, stride=B), :] = value

    scale = close(store_west)
    west_shift = []
    for k in range(3):
        rows = pl.ds(k * 512, 512)
        west_send[rows, :] = (inter[rows, :] * scale).astype(BF)
        west_shift.append(
            pltpu.make_async_remote_copy(
                src_ref=west_send.at[rows], dst_ref=west_recv.at[rows], send_sem=wsend.at[k], recv_sem=wrecv.at[k],
                device_id=east, device_id_type=MESH,
            )
        )
        west_shift[k].start()
    chain(1, 1)
    for copy in last_corners:
        copy.start()
    contract(west_recv, west_shift)

    def store_last(r, value):
        fin[r, 0:CHI, :] = value

    scale = close(store_last)

    @pl.when(mirror)
    def _():
        e_fin[...] = jnp.concatenate([(fin[r].T[0:CHI, 0:CHI] * scale).astype(BF) for r in range(B)], axis=1)

    @pl.when(jnp.logical_not(mirror))
    def _():
        e_fin[...] = jnp.concatenate([(fin[r, 0:CHI, 0:CHI] * scale).astype(BF) for r in range(B)], axis=1)

    edge_shift = remote(e_fin, e_out.at[0, 0], 9, east)
    edge_shift.start()
    for copy in last_corners + [edge_shift]:
        copy.wait_recv()
    for copy in last_corners + west_shift + [edge_shift, corner_send(0), corner_send(1)] + first_sends[2:]:
        copy.wait_send()
    if spread:
        @pl.when(jnp.logical_not(first))
        def _():
            first_sends[0].wait_send()

        @pl.when(jnp.logical_not(last))
        def _():
            first_sends[1].wait_send()

        @pl.when(helper)
        def _():
            for copy in forwards():
                copy.wait_send()
    else:
        first_sends[0].wait_send()
        first_sends[1].wait_send()


def settle(*refs):
    sources, targets, stages, sem = refs[0:3], refs[3:6], refs[6:9], refs[9]
    fetch = [pltpu.make_async_copy(sources[i], stages[i], sem.at[i]) for i in range(3)]
    keep = [pltpu.make_async_copy(stages[i], targets[i], sem.at[3 + i]) for i in range(3)]
    for copy in fetch:
        copy.start()
    for i in (0, 2, 1):
        fetch[i].wait()
        keep[i].start()
    for copy in keep:
        copy.wait()


def per_device(c_upper, edge_upper, edge_left, c_lower, edge_lower, site_ket, time_gate, quench_sites):
    hbm = pl.BlockSpec(memory_space=pl.ANY)
    vmem = pl.BlockSpec(memory_space=pltpu.VMEM)
    smem = pl.BlockSpec(memory_space=pltpu.SMEM)
    corner = jax.ShapeDtypeStruct((1, 1, CHI, CHI), BF)
    edge = jax.ShapeDtypeStruct((1, 1, CHI, B * CHI), BF)
    inner = pltpu.VMEM((CHI * B, L), BF)
    four = pltpu.VMEM((4, L, L), BF)
    two_edges = pltpu.VMEM((2, CHI, B * CHI), BF)
    two_tall = pltpu.VMEM((2, B * L, L), BF)
    dma = pltpu.SemaphoreType.DMA
    moved = pl.pallas_call(
        kernel,
        out_shape=(corner, edge, corner),
        in_specs=[hbm] * 5 + [vmem, smem, smem],
        out_specs=(hbm,) * 3,
        scratch_shapes=[
            two_edges, two_edges, pltpu.VMEM((CHI, B * CHI), BF), pltpu.VMEM((4, CHI, CHI), BF),
            two_tall, two_tall, four, four, four, pltpu.VMEM((256, 256), BF),
            inner, inner, inner, pltpu.VMEM((3 * L, B * L), BF), pltpu.VMEM((CHI * B, L), F32),
            pltpu.VMEM((CHI, CHI * B), BF), pltpu.VMEM((B * L, L), BF), pltpu.VMEM((6, B, 256, L), BF),
            pltpu.VMEM((8, CHI * B, 2 * L), BF), pltpu.VMEM((B, L, L), F32),
            pltpu.VMEM((CHI, B * CHI), BF), pltpu.VMEM((2, CHI, CHI), BF),
            pltpu.VMEM((2, CHI, L), BF),
            dma((5,)), dma((10,)), dma((10,)), dma((CHUNKS,)), dma((2,)), dma((3,)), dma((3,)),
            pltpu.SemaphoreType.REGULAR,
        ],
        compiler_params=pltpu.CompilerParams(
            collective_id=0, has_side_effects=True, vmem_limit_bytes=63 * 1024 * 1024
        ),
        name="left_move",
    )(c_upper, edge_upper, edge_left, c_lower, edge_lower, site_ket, time_gate, quench_sites)
    return pl.pallas_call(
        settle,
        out_shape=(corner, edge, corner),
        in_specs=[hbm] * 3,
        out_specs=(hbm,) * 3,
        scratch_shapes=[
            pltpu.VMEM((1, 1, CHI, CHI), BF), pltpu.VMEM((1, 1, CHI, B * CHI), BF), pltpu.VMEM((1, 1, CHI, CHI), BF),
            pltpu.SemaphoreType.DMA((6,)),
        ],
        compiler_params=pltpu.CompilerParams(vmem_limit_bytes=63 * 1024 * 1024),
        name="settle",
    )(*moved)


def solution(mesh):
    site = P("gx", "gy", None, None)
    return jax.shard_map(
        per_device,
        mesh=mesh,
        in_specs=(site,) * 6 + (P(), P()),
        out_specs=(site,) * 3,
        check_vma=False,
    )
```

```python
import jax
import jax.numpy as jnp
from jax import lax
from jax.experimental import pallas as pl
from jax.experimental.pallas import tpu as pltpu
from jax.sharding import PartitionSpec as P

NS_ITERS = 6
STEPS = 2
MESH = pl.DeviceIdType.MESH
CHI = 96
B = 16
HALF = 16
CHUNKS = 12
L = 128
F32 = jnp.float32
BF = jnp.bfloat16


def nt(a, b):
    return lax.dot_general(a, b, (((1,), (1,)), ((), ())), preferred_element_type=F32)


def nn(a, b):
    return jnp.dot(a, b, preferred_element_type=F32)


def split(x):
    hi = x.astype(BF)
    return hi, (x - hi.astype(F32)).astype(BF)


def product(a, b):
    a_hi, a_lo = split(a)
    b_hi, b_lo = split(b)
    return nn(
        jnp.concatenate([a_hi, a_lo], axis=1), jnp.concatenate([b_hi, b_hi], axis=0)
    ) + nn(a_hi, b_lo)


def eye():
    row = lax.broadcasted_iota(jnp.int32, (L, L), 0)
    col = lax.broadcasted_iota(jnp.int32, (L, L), 1)
    return jnp.where((row == col) & (row < CHI), 1.0, 0.0).astype(F32)


def polar_right(gram):
    one = eye()
    scale = 1.0 / (jnp.sum(gram * one) + 1e-06)
    s = gram * scale
    p = 1.5 * one - 0.5 * s
    m = p
    for _ in range(NS_ITERS - 1):
        s = product(product(s, p), p)
        p = 1.5 * one - 0.5 * s
        m = product(m, p)
    return m * jnp.sqrt(scale)


def unit_corner(x):
    return (x * lax.rsqrt(jnp.sum(x * x) * (1.0 / (CHI * CHI)) + 1e-06)).astype(BF)


def transposed_edge(edge_ref, out_ref):
    for chunk in range(4):
        lanes = edge_ref[:, chunk * 384 : (chunk + 1) * 384]
        lanes = jnp.concatenate([lanes, jnp.zeros((L - CHI, 384), BF)], axis=0)
        turned = lanes.T
        for i in range(4):
            d = chunk * 4 + i
            out_ref[d * L : d * L + CHI, :] = turned[i * CHI : (i + 1) * CHI, :]
            out_ref[d * L + CHI : (d + 1) * L, :] = jnp.zeros((L - CHI, L), BF)


def double_layer(ket_ref, gate_ref, quench_ref, own_index, mirror, out_ref):
    n = lax.broadcasted_iota(jnp.int32, (256, 256), 0)
    m = lax.broadcasted_iota(jnp.int32, (256, 256), 1)
    f4 = lambda x, k: (x >> (6 - 2 * k)) & 3
    outer = jnp.where(mirror, f4(m, 3), f4(m, 1))
    inner = jnp.where(mirror, f4(n, 1), f4(n, 3))
    ket_mask = (f4(n, 2) == outer) & (f4(n, 0) == f4(m, 2))
    bra_mask = (f4(n, 3) == outer) & (f4(n, 1) == f4(m, 2))
    ket_spread = ((f4(n, 0) == f4(m, 2)) & (inner == f4(m, 0))).astype(F32).astype(BF)
    bra_spread = ((f4(n, 0) == f4(m, 3)) & (inner == f4(m, 1))).astype(F32).astype(BF)
    chosen = quench_ref[0] == own_index
    for i in range(1, 4):
        chosen = chosen | (quench_ref[i] == own_index)
    kets = [ket_ref[0, 0, s : s + 1, :].astype(F32) for s in range(2)]
    total = jnp.zeros((256, 256), F32)
    for s in range(2):
        bra = jnp.zeros((1, 256), F32)
        for t in range(2):
            gram = gate_ref[0, s] * gate_ref[0, t] + gate_ref[1, s] * gate_ref[1, t]
            weight = jnp.where(chosen, gram, 1.0 if s == t else 0.0)
            bra = bra + weight * kets[t]
        bra = bra.astype(BF).astype(F32)
        ket_part = nn(jnp.where(ket_mask, kets[s], 0.0).astype(BF), ket_spread)
        bra_part = nn(jnp.where(bra_mask, bra, 0.0).astype(BF), bra_spread)
        total = total + ket_part * bra_part
    out_ref[...] = total.astype(BF)


def kernel(
    c_up_in, e_up_in, e_left_in, c_low_in, e_low_in, ket_ref, gate_ref, quench_ref,
    c_up_out, e_out, c_low_out,
    own, near, west_nat, c_in, et_own, et_near, cpad, c_send, c_recv, w_ref,
    west, west_recv, west_send, glu, inter, pup, pt, fs, t_ref, fin, e_fin, c_fin,
    hop, lsem, ssem, rsem, psem, hsem, wsend, wrecv, ready,
):
    gx, gy = lax.axis_index("gx"), lax.axis_index("gy")
    ncol, nrow = lax.axis_size("gx"), lax.axis_size("gy")
    north = (gx, lax.rem(gy + nrow - 1, nrow))
    south = (gx, lax.rem(gy + 1, nrow))
    east = (lax.rem(gx + 1, ncol), gy)
    before = (lax.rem(gx + ncol - 1, ncol), gy)
    spread = nrow == 2 * HALF
    period = HALF if spread else nrow
    half, place = gy // period, lax.rem(gy, period)
    first, last = place == 0, place == period - 1
    helper = (place >= 2) & (place < 2 + CHUNKS)
    mirror = last
    flip = jnp.where(mirror, 1, 0)
    barrier = pltpu.get_barrier_semaphore()

    def greet(peer):
        pl.semaphore_signal(barrier, inc=1, device_id=peer, device_id_type=MESH)

    edge_row = first | last
    far = jnp.where(first, (1 - half) * HALF + HALF - 1, (1 - half) * HALF)
    greet(before)
    if spread:
        @pl.when(jnp.logical_not(first & (half == 1)))
        def _():
            greet(north)

        @pl.when(jnp.logical_not(last & (half == 1)))
        def _():
            greet(south)

        @pl.when(edge_row & (half == 0))
        def _():
            for c in range(CHUNKS):
                greet((gx, HALF + 2 + c))

        @pl.when(helper)
        def _():
            greet((gx, half * HALF))
            greet((gx, half * HALF + HALF - 1))

        @pl.when(helper & (half == 0))
        def _():
            greet((gx, HALF))
            greet((gx, 2 * HALF - 1))

        greeted = (
            3
            + jnp.where(helper & (half == 1), 2, 0)
            + jnp.where(edge_row, CHUNKS, 0)
            + jnp.where(edge_row & (half == 1), CHUNKS, 0)
            - jnp.where(edge_row & (half == 0), 1, 0)
        )
    else:
        greet(north)
        greet(south)
        greeted = 3

    local = [
        pltpu.make_async_copy(src.at[0, 0], dst, lsem.at[i])
        for i, (src, dst) in enumerate((
            (e_low_in, own.at[flip]), (e_up_in, own.at[1 - flip]), (e_left_in, west_nat),
            (c_low_in, c_in.at[2 * flip]), (c_up_in, c_in.at[2 - 2 * flip]),
        ))
    ]
    for copy in local:
        copy.start()
    pl.semaphore_wait(barrier, greeted)
    if spread:
        @pl.when(edge_row & (half == 1))
        def _():
            for row in [far] + [2 + c for c in range(CHUNKS)]:
                pl.semaphore_signal(ready, inc=1, device_id=(gx, row), device_id_type=MESH)


    def remote(src, dst, i, peer, j=None):
        return pltpu.make_async_remote_copy(
            src_ref=src, dst_ref=dst, send_sem=ssem.at[i], recv_sem=rsem.at[i if j is None else j],
            device_id=peer, device_id_type=MESH,
        )

    to_north = jnp.where(first, 1, 0)
    to_south = jnp.where(place == period - 2, 0, 1)
    first_sends = [
        remote(e_up_in.at[0, 0], near.at[to_north], 0, north, to_north),
        remote(e_low_in.at[0, 0], near.at[to_south], 1, south, to_south),
        remote(c_up_in.at[0, 0], c_in.at[1 + 2 * to_north], 2, north, 2 + to_north),
        remote(c_low_in.at[0, 0], c_in.at[1 + 2 * to_south], 3, south, 2 + to_south),
    ]

    def relay(src, dst, send, recv, peer):
        return pltpu.make_async_remote_copy(
            src_ref=src, dst_ref=dst, send_sem=psem.at[send], recv_sem=recv,
            device_id=peer, device_id_type=MESH,
        )

    def chunk_sends(edge_in, slot):
        return [
            relay(edge_in.at[0, 0, :, pl.ds(c * L, L)], hop.at[slot], c, hsem.at[slot], (gx, half * HALF + 2 + c))
            for c in range(CHUNKS)
        ]

    lanes = pl.ds(pl.multiple_of((place - 2) * L, L), L)

    def forwards():
        return [
            relay(hop.at[0], near.at[1, :, lanes], 0, rsem.at[1], (gx, (1 - half) * HALF + HALF - 1)),
            relay(hop.at[1], near.at[1, :, lanes], 1, rsem.at[1], (gx, (1 - half) * HALF)),
        ]

    def forward():
        @pl.when(half == 0)
        def _():
            pl.semaphore_wait(ready, 2)

        for slot, copy in enumerate(forwards()):
            relay(hop.at[slot], hop.at[slot], slot, hsem.at[slot], north).wait_recv()
            copy.start()

    if spread:
        @pl.when(jnp.logical_not(first & (half == 0)))
        def _():
            first_sends[2].start()

        @pl.when(jnp.logical_not(last & (half == 0)))
        def _():
            first_sends[3].start()

        def near_sends(side):
            @pl.when(jnp.logical_not(first) & (half == side))
            def _():
                first_sends[0].start()

            @pl.when(jnp.logical_not(last) & (half == side))
            def _():
                first_sends[1].start()

        near_sends(0)

        @pl.when(first)
        def _():
            copies = chunk_sends(e_up_in, 0)
            for copy in copies:
                copy.start()
            for copy in copies:
                copy.wait_send()

        @pl.when(last)
        def _():
            copies = chunk_sends(e_low_in, 1)
            for copy in copies:
                copy.start()
            for copy in copies:
                copy.wait_send()

        @pl.when(helper & (half == 1))
        def _():
            forward()

        near_sends(1)
    else:
        for copy in first_sends:
            copy.start()

    double_layer(ket_ref, gate_ref, quench_ref, gx * nrow + gy, mirror, w_ref)
    for copy in local:
        copy.wait()
    for cut in (0, 1):
        transposed_edge(own.at[cut], et_own.at[cut])

    def interleave(turned):
        for l in range(B):
            value = jnp.concatenate(
                [west_nat[:, l * CHI : (l + 1) * CHI].astype(F32), jnp.zeros((CHI, L - CHI), F32)], axis=1
            )
            if turned:
                value = jnp.concatenate([value, jnp.zeros((L - CHI, L), F32)], axis=0).T[0:CHI, :]
            inter[pl.ds(l, CHI, stride=B), :] = value

    @pl.when(mirror)
    def _():
        interleave(True)

    @pl.when(jnp.logical_not(mirror))
    def _():
        interleave(False)

    west[...] = inter[...].astype(BF)

    def arrive(cut):
        remote(near.at[cut], near.at[cut], cut, north).wait_recv()
        remote(c_in.at[0], c_in.at[0], 2 + cut, north).wait_recv()
        for i in (2 * cut, 2 * cut + 1):
            cpad[i] = jnp.zeros((L, L), BF)
            cpad[i, 0:CHI, :] = jnp.concatenate([c_in[i], jnp.zeros((CHI, L - CHI), BF)], axis=1)
        transposed_edge(near.at[cut], et_near.at[cut])

    def corner_send(cut):
        pair = pl.ds(2 * cut, 2)
        return remote(c_send.at[pair], c_recv.at[pair], 4 + cut, east)

    last_corners = [
        remote(c_fin.at[flip], c_low_out.at[0, 0], 7, east),
        remote(c_fin.at[1 - flip], c_up_out.at[0, 0], 8, east),
    ]

    def chain(step, cut):
        if step == 0:
            arrive(cut)
        else:
            corner_send(cut).wait_recv()
        corners = cpad if step == 0 else c_recv
        for piece in range(8):
            rows = slice(piece * 256, (piece + 1) * 256)
            mine = nt(et_own[cut, rows, :], corners[2 * cut])
            other = nt(et_near[cut, rows, :], corners[2 * cut + 1])
            for i, value in enumerate(((mine + other), mine, other)):
                value = value.astype(BF)
                for side in range(2):
                    at = piece * 256 + side * L
                    glu[i * L : (i + 1) * L, at : at + L] = value[side * L : (side + 1) * L, :]
        sums = nt(glu[0:L, :], glu[...])
        if cut == 1:
            for d in range(B):
                rows = slice(d * L, (d + 1) * L)
                value = nt(corners[2], et_own[1, rows, :]) + nt(corners[3], et_near[1, rows, :])
                inter[pl.ds(d, CHI, stride=B), :] = value[0:CHI, :]
        m = polar_right(sums[:, 0:L])
        new_own = unit_corner(product(m, sums[:, L : 2 * L]))
        if step < STEPS - 1:
            c_send[2 * cut] = new_own
            c_send[2 * cut + 1] = unit_corner(product(m, sums[:, 2 * L : 3 * L]))
            corner_send(cut).start()
        else:
            c_fin[cut] = new_own[0:CHI, 0:CHI]
        m_rows = jnp.concatenate(list(split(m)), axis=0)
        if cut == 0:
            for piece in range(8):
                both = nn(m_rows, glu[0:L, piece * 256 : (piece + 1) * 256])
                both = (both[0:L] + both[L : 2 * L]).astype(BF)
                for side in range(2):
                    at = piece * 256 + side * L
                    pt[at : at + L, :] = both[:, side * L : (side + 1) * L]
        else:
            for piece in range(6):
                rows = slice(piece * 256, (piece + 1) * 256)
                both = nt(m_rows, inter[rows, :].astype(BF))
                pup[:, rows] = (both[0:CHI] + both[L : L + CHI]).astype(BF)

    def contract(left, arrivals=None):
        def spread_rows(k):
            if arrivals is not None and k % 2 == 0:
                arrivals[k // 2].wait_recv()
            rows = left[k * 256 : (k + 1) * 256, :]
            for pair in range(8):
                out = nt(rows, pt[pair * 256 : (pair + 1) * 256, :]).astype(BF)
                fs[k, 2 * pair] = out[:, 0:L]
                fs[k, 2 * pair + 1] = out[:, L : 2 * L]

        def absorb(k):
            for pair in range(8):
                cols = [
                    jnp.concatenate([fs[k, d, u * B : (u + 1) * B, :] for d in range(B)], axis=0)
                    for u in (2 * pair, 2 * pair + 1)
                ]
                out = nn(w_ref[...], jnp.concatenate(cols, axis=1)).astype(BF)
                for side in range(2):
                    at = k * 256 + (2 * pair + side) * B
                    for r in range(B):
                        t_ref[r // 2, at : at + B, (r % 2) * L : (r % 2 + 1) * L] = out[
                            r * B : (r + 1) * B, side * L : (side + 1) * L
                        ]

        spread_rows(0)
        for k in range(6):
            if k < 5:
                spread_rows(k + 1)
            absorb(k)

    def close(store):
        square = jnp.zeros((CHI, CHI), F32)
        for pair in range(8):
            out = nn(pup[...], t_ref[pair])
            for side in range(2):
                value = out[:, side * L : side * L + CHI]
                square = square + value * value
                store(2 * pair + side, jnp.concatenate([value, jnp.zeros((CHI, L - CHI), F32)], axis=1))
        return lax.rsqrt(jnp.sum(square) * (1.0 / (CHI * CHI * B)) + 1e-06)

    chain(0, 0)
    contract(west)

    @pl.when(edge_row)
    def _():
        chain(1, 0)

    if spread:
        @pl.when(first & (half == 0))
        def _():
            pl.semaphore_wait(ready, 1)
            first_sends[2].start()

        @pl.when(last & (half == 0))
        def _():
            pl.semaphore_wait(ready, 1)
            first_sends[3].start()

    chain(0, 1)
    if spread:
        @pl.when(helper & (half == 0))
        def _():
            forward()

    def store_west(r, value):
        inter[pl.ds(r, CHI, stride=B), :] = value

    scale = close(store_west)
    west_shift = []
    for k in range(3):
        rows = pl.ds(k * 512, 512)
        west_send[rows, :] = (inter[rows, :] * scale).astype(BF)
        west_shift.append(
            pltpu.make_async_remote_copy(
                src_ref=west_send.at[rows], dst_ref=west_recv.at[rows], send_sem=wsend.at[k], recv_sem=wrecv.at[k],
                device_id=east, device_id_type=MESH,
            )
        )
        west_shift[k].start()

    @pl.when(jnp.logical_not(edge_row))
    def _():
        chain(1, 0)

    chain(1, 1)
    for copy in last_corners:
        copy.start()
    contract(west_recv, west_shift)

    def store_last(r, value):
        fin[r, 0:CHI, :] = value

    scale = close(store_last)

    @pl.when(mirror)
    def _():
        e_fin[...] = jnp.concatenate([(fin[r].T[0:CHI, 0:CHI] * scale).astype(BF) for r in range(B)], axis=1)

    @pl.when(jnp.logical_not(mirror))
    def _():
        e_fin[...] = jnp.concatenate([(fin[r, 0:CHI, 0:CHI] * scale).astype(BF) for r in range(B)], axis=1)

    edge_shift = remote(e_fin, e_out.at[0, 0], 9, east)
    edge_shift.start()
    for copy in last_corners + [edge_shift]:
        copy.wait_recv()
    for copy in last_corners + west_shift + [edge_shift, corner_send(0), corner_send(1)] + first_sends[2:]:
        copy.wait_send()
    if spread:
        @pl.when(jnp.logical_not(first))
        def _():
            first_sends[0].wait_send()

        @pl.when(jnp.logical_not(last))
        def _():
            first_sends[1].wait_send()

        @pl.when(helper)
        def _():
            for copy in forwards():
                copy.wait_send()
    else:
        first_sends[0].wait_send()
        first_sends[1].wait_send()


def settle(*refs):
    sources, targets, stages, sem = refs[0:3], refs[3:6], refs[6:9], refs[9]
    fetch = [pltpu.make_async_copy(sources[i], stages[i], sem.at[i]) for i in range(3)]
    keep = [pltpu.make_async_copy(stages[i], targets[i], sem.at[3 + i]) for i in range(3)]
    for copy in fetch:
        copy.start()
    for i in (0, 2, 1):
        fetch[i].wait()
        keep[i].start()
    for copy in keep:
        copy.wait()


def per_device(c_upper, edge_upper, edge_left, c_lower, edge_lower, site_ket, time_gate, quench_sites):
    hbm = pl.BlockSpec(memory_space=pl.ANY)
    vmem = pl.BlockSpec(memory_space=pltpu.VMEM)
    smem = pl.BlockSpec(memory_space=pltpu.SMEM)
    corner = jax.ShapeDtypeStruct((1, 1, CHI, CHI), BF)
    edge = jax.ShapeDtypeStruct((1, 1, CHI, B * CHI), BF)
    inner = pltpu.VMEM((CHI * B, L), BF)
    four = pltpu.VMEM((4, L, L), BF)
    two_edges = pltpu.VMEM((2, CHI, B * CHI), BF)
    two_tall = pltpu.VMEM((2, B * L, L), BF)
    dma = pltpu.SemaphoreType.DMA
    moved = pl.pallas_call(
        kernel,
        out_shape=(corner, edge, corner),
        in_specs=[hbm] * 5 + [vmem, smem, smem],
        out_specs=(hbm,) * 3,
        scratch_shapes=[
            two_edges, two_edges, pltpu.VMEM((CHI, B * CHI), BF), pltpu.VMEM((4, CHI, CHI), BF),
            two_tall, two_tall, four, four, four, pltpu.VMEM((256, 256), BF),
            inner, inner, inner, pltpu.VMEM((3 * L, B * L), BF), pltpu.VMEM((CHI * B, L), F32),
            pltpu.VMEM((CHI, CHI * B), BF), pltpu.VMEM((B * L, L), BF), pltpu.VMEM((6, B, 256, L), BF),
            pltpu.VMEM((8, CHI * B, 2 * L), BF), pltpu.VMEM((B, L, L), F32),
            pltpu.VMEM((CHI, B * CHI), BF), pltpu.VMEM((2, CHI, CHI), BF),
            pltpu.VMEM((2, CHI, L), BF),
            dma((5,)), dma((10,)), dma((10,)), dma((CHUNKS,)), dma((2,)), dma((3,)), dma((3,)),
            pltpu.SemaphoreType.REGULAR,
        ],
        compiler_params=pltpu.CompilerParams(
            collective_id=0, has_side_effects=True, vmem_limit_bytes=63 * 1024 * 1024
        ),
        name="left_move",
    )(c_upper, edge_upper, edge_left, c_lower, edge_lower, site_ket, time_gate, quench_sites)
    return pl.pallas_call(
        settle,
        out_shape=(corner, edge, corner),
        in_specs=[hbm] * 3,
        out_specs=(hbm,) * 3,
        scratch_shapes=[
            pltpu.VMEM((1, 1, CHI, CHI), BF), pltpu.VMEM((1, 1, CHI, B * CHI), BF), pltpu.VMEM((1, 1, CHI, CHI), BF),
            pltpu.SemaphoreType.DMA((6,)),
        ],
        compiler_params=pltpu.CompilerParams(vmem_limit_bytes=63 * 1024 * 1024),
        name="settle",
    )(*moved)


def solution(mesh):
    site = P("gx", "gy", None, None)
    return jax.shard_map(
        per_device,
        mesh=mesh,
        in_specs=(site,) * 6 + (P(), P()),
        out_specs=(site,) * 3,
        check_vma=False,
    )
```

```python
import jax
import jax.numpy as jnp
from jax import lax
from jax.experimental import pallas as pl
from jax.experimental.pallas import tpu as pltpu
from jax.sharding import PartitionSpec as P

NS_ITERS = 6
STEPS = 2
MESH = pl.DeviceIdType.MESH
CHI = 96
B = 16
HALF = 16
CHUNKS = 12
L = 128
F32 = jnp.float32
BF = jnp.bfloat16


def nt(a, b):
    return lax.dot_general(a, b, (((1,), (1,)), ((), ())), preferred_element_type=F32)


def nn(a, b):
    return jnp.dot(a, b, preferred_element_type=F32)


def split(x):
    hi = x.astype(BF)
    return hi, (x - hi.astype(F32)).astype(BF)


def product(a, b):
    a_hi, a_lo = split(a)
    b_hi, b_lo = split(b)
    return nn(
        jnp.concatenate([a_hi, a_lo], axis=1), jnp.concatenate([b_hi, b_hi], axis=0)
    ) + nn(a_hi, b_lo)


def eye():
    row = lax.broadcasted_iota(jnp.int32, (L, L), 0)
    col = lax.broadcasted_iota(jnp.int32, (L, L), 1)
    return jnp.where((row == col) & (row < CHI), 1.0, 0.0).astype(F32)


def polar_right(gram):
    one = eye()
    scale = 1.0 / (jnp.sum(gram * one) + 1e-06)
    s = gram * scale
    p = 1.5 * one - 0.5 * s
    m = p
    for _ in range(NS_ITERS - 1):
        s = product(product(s, p), p)
        p = 1.5 * one - 0.5 * s
        m = product(m, p)
    return m * jnp.sqrt(scale)


def unit_corner(x):
    return (x * lax.rsqrt(jnp.sum(x * x) * (1.0 / (CHI * CHI)) + 1e-06)).astype(BF)


def transposed_edge(edge_ref, out_ref):
    for chunk in range(4):
        lanes = edge_ref[:, chunk * 384 : (chunk + 1) * 384]
        lanes = jnp.concatenate([lanes, jnp.zeros((L - CHI, 384), BF)], axis=0)
        turned = lanes.T
        for i in range(4):
            d = chunk * 4 + i
            out_ref[d * L : d * L + CHI, :] = turned[i * CHI : (i + 1) * CHI, :]
            out_ref[d * L + CHI : (d + 1) * L, :] = jnp.zeros((L - CHI, L), BF)


def double_layer(ket_ref, gate_ref, quench_ref, own_index, mirror, out_ref):
    n = lax.broadcasted_iota(jnp.int32, (256, 256), 0)
    m = lax.broadcasted_iota(jnp.int32, (256, 256), 1)
    f4 = lambda x, k: (x >> (6 - 2 * k)) & 3
    outer = jnp.where(mirror, f4(m, 3), f4(m, 1))
    inner = jnp.where(mirror, f4(n, 1), f4(n, 3))
    ket_mask = (f4(n, 2) == outer) & (f4(n, 0) == f4(m, 2))
    bra_mask = (f4(n, 3) == outer) & (f4(n, 1) == f4(m, 2))
    ket_spread = ((f4(n, 0) == f4(m, 2)) & (inner == f4(m, 0))).astype(F32).astype(BF)
    bra_spread = ((f4(n, 0) == f4(m, 3)) & (inner == f4(m, 1))).astype(F32).astype(BF)
    chosen = quench_ref[0] == own_index
    for i in range(1, 4):
        chosen = chosen | (quench_ref[i] == own_index)
    kets = [ket_ref[0, 0, s : s + 1, :].astype(F32) for s in range(2)]
    total = jnp.zeros((256, 256), F32)
    for s in range(2):
        bra = jnp.zeros((1, 256), F32)
        for t in range(2):
            gram = gate_ref[0, s] * gate_ref[0, t] + gate_ref[1, s] * gate_ref[1, t]
            weight = jnp.where(chosen, gram, 1.0 if s == t else 0.0)
            bra = bra + weight * kets[t]
        bra = bra.astype(BF).astype(F32)
        ket_part = nn(jnp.where(ket_mask, kets[s], 0.0).astype(BF), ket_spread)
        bra_part = nn(jnp.where(bra_mask, bra, 0.0).astype(BF), bra_spread)
        total = total + ket_part * bra_part
    out_ref[...] = total.astype(BF)


def kernel(
    c_up_in, e_up_in, e_left_in, c_low_in, e_low_in, ket_ref, gate_ref, quench_ref,
    c_up_out, e_out, c_low_out,
    own, near, west_nat, c_in, et_own, et_near, cpad, c_send, c_recv, w_ref,
    west, west_recv, west_send, glu, inter, pup, pt, fs, t_ref, fin, e_fin, c_fin,
    hop, lsem, ssem, rsem, psem, hsem, wsend, wrecv, ready,
):
    gx, gy = lax.axis_index("gx"), lax.axis_index("gy")
    ncol, nrow = lax.axis_size("gx"), lax.axis_size("gy")
    north = (gx, lax.rem(gy + nrow - 1, nrow))
    south = (gx, lax.rem(gy + 1, nrow))
    east = (lax.rem(gx + 1, ncol), gy)
    before = (lax.rem(gx + ncol - 1, ncol), gy)
    spread = nrow == 2 * HALF
    period = HALF if spread else nrow
    half, place = gy // period, lax.rem(gy, period)
    first, last = place == 0, place == period - 1
    helper = (place >= 2) & (place < 2 + CHUNKS)
    mirror = last
    flip = jnp.where(mirror, 1, 0)
    barrier = pltpu.get_barrier_semaphore()

    def greet(peer):
        pl.semaphore_signal(barrier, inc=1, device_id=peer, device_id_type=MESH)

    edge_row = first | last
    far = jnp.where(first, (1 - half) * HALF + HALF - 1, (1 - half) * HALF)
    greet(before)
    if spread:
        @pl.when(jnp.logical_not(first & (half == 1)))
        def _():
            greet(north)

        @pl.when(jnp.logical_not(last & (half == 1)))
        def _():
            greet(south)

        @pl.when(edge_row & (half == 0))
        def _():
            for c in range(CHUNKS):
                greet((gx, HALF + 2 + c))

        @pl.when(helper)
        def _():
            greet((gx, half * HALF))
            greet((gx, half * HALF + HALF - 1))

        @pl.when(helper & (half == 0))
        def _():
            greet((gx, HALF))
            greet((gx, 2 * HALF - 1))

        greeted = (
            3
            + jnp.where(helper & (half == 1), 2, 0)
            + jnp.where(edge_row, CHUNKS, 0)
            + jnp.where(edge_row & (half == 1), CHUNKS, 0)
            - jnp.where(edge_row & (half == 0), 1, 0)
        )
    else:
        greet(north)
        greet(south)
        greeted = 3

    local = [
        pltpu.make_async_copy(src.at[0, 0], dst, lsem.at[i])
        for i, (src, dst) in enumerate((
            (e_low_in, own.at[flip]), (e_up_in, own.at[1 - flip]), (e_left_in, west_nat),
            (c_low_in, c_in.at[2 * flip]), (c_up_in, c_in.at[2 - 2 * flip]),
        ))
    ]
    for copy in local:
        copy.start()
    pl.semaphore_wait(barrier, greeted)
    if spread:
        @pl.when(edge_row & (half == 1))
        def _():
            for row in [far] + [2 + c for c in range(CHUNKS)]:
                pl.semaphore_signal(ready, inc=1, device_id=(gx, row), device_id_type=MESH)


    def remote(src, dst, i, peer, j=None):
        return pltpu.make_async_remote_copy(
            src_ref=src, dst_ref=dst, send_sem=ssem.at[i], recv_sem=rsem.at[i if j is None else j],
            device_id=peer, device_id_type=MESH,
        )

    to_north = jnp.where(first, 1, 0)
    to_south = jnp.where(place == period - 2, 0, 1)
    first_sends = [
        remote(e_up_in.at[0, 0], near.at[to_north], 0, north, to_north),
        remote(e_low_in.at[0, 0], near.at[to_south], 1, south, to_south),
        remote(c_up_in.at[0, 0], c_in.at[1 + 2 * to_north], 2, north, 2 + to_north),
        remote(c_low_in.at[0, 0], c_in.at[1 + 2 * to_south], 3, south, 2 + to_south),
    ]

    def relay(src, dst, send, recv, peer):
        return pltpu.make_async_remote_copy(
            src_ref=src, dst_ref=dst, send_sem=psem.at[send], recv_sem=recv,
            device_id=peer, device_id_type=MESH,
        )

    def chunk_sends(edge_in, slot):
        return [
            relay(edge_in.at[0, 0, :, pl.ds(c * L, L)], hop.at[slot], c, hsem.at[slot], (gx, half * HALF + 2 + c))
            for c in range(CHUNKS)
        ]

    lanes = pl.ds(pl.multiple_of((place - 2) * L, L), L)

    def forwards():
        return [
            relay(hop.at[0], near.at[1, :, lanes], 0, rsem.at[1], (gx, (1 - half) * HALF + HALF - 1)),
            relay(hop.at[1], near.at[1, :, lanes], 1, rsem.at[1], (gx, (1 - half) * HALF)),
        ]

    def forward():
        @pl.when(half == 0)
        def _():
            pl.semaphore_wait(ready, 2)

        for slot, copy in enumerate(forwards()):
            relay(hop.at[slot], hop.at[slot], slot, hsem.at[slot], north).wait_recv()
            copy.start()

    if spread:
        @pl.when(jnp.logical_not(first & (half == 0)))
        def _():
            first_sends[2].start()

        @pl.when(jnp.logical_not(last & (half == 0)))
        def _():
            first_sends[3].start()

        def near_sends(side):
            @pl.when(jnp.logical_not(first) & (half == side))
            def _():
                first_sends[0].start()

            @pl.when(jnp.logical_not(last) & (half == side))
            def _():
                first_sends[1].start()

        near_sends(0)

        @pl.when(first)
        def _():
            copies = chunk_sends(e_up_in, 0)
            for copy in copies:
                copy.start()
            for copy in copies:
                copy.wait_send()

        @pl.when(last)
        def _():
            copies = chunk_sends(e_low_in, 1)
            for copy in copies:
                copy.start()
            for copy in copies:
                copy.wait_send()

        @pl.when(helper & (half == 1))
        def _():
            forward()

        near_sends(1)
    else:
        for copy in first_sends:
            copy.start()

    double_layer(ket_ref, gate_ref, quench_ref, gx * nrow + gy, mirror, w_ref)
    for copy in local:
        copy.wait()
    for cut in (0, 1):
        transposed_edge(own.at[cut], et_own.at[cut])

    def interleave(turned):
        for l in range(B):
            value = jnp.concatenate(
                [west_nat[:, l * CHI : (l + 1) * CHI].astype(F32), jnp.zeros((CHI, L - CHI), F32)], axis=1
            )
            if turned:
                value = jnp.concatenate([value, jnp.zeros((L - CHI, L), F32)], axis=0).T[0:CHI, :]
            inter[pl.ds(l, CHI, stride=B), :] = value

    @pl.when(mirror)
    def _():
        interleave(True)

    @pl.when(jnp.logical_not(mirror))
    def _():
        interleave(False)

    west[...] = inter[...].astype(BF)

    def arrive(cut):
        remote(near.at[cut], near.at[cut], cut, north).wait_recv()
        remote(c_in.at[0], c_in.at[0], 2 + cut, north).wait_recv()
        for i in (2 * cut, 2 * cut + 1):
            cpad[i] = jnp.zeros((L, L), BF)
            cpad[i, 0:CHI, :] = jnp.concatenate([c_in[i], jnp.zeros((CHI, L - CHI), BF)], axis=1)
        transposed_edge(near.at[cut], et_near.at[cut])

    def corner_send(cut):
        pair = pl.ds(2 * cut, 2)
        return remote(c_send.at[pair], c_recv.at[pair], 4 + cut, east)

    last_corners = [
        remote(c_fin.at[flip], c_low_out.at[0, 0], 7, east),
        remote(c_fin.at[1 - flip], c_up_out.at[0, 0], 8, east),
    ]

    def chain(step, cut):
        if step == 0:
            arrive(cut)
        else:
            corner_send(cut).wait_recv()
        corners = cpad if step == 0 else c_recv
        for piece in range(8):
            rows = slice(piece * 256, (piece + 1) * 256)
            mine = nt(et_own[cut, rows, :], corners[2 * cut])
            other = nt(et_near[cut, rows, :], corners[2 * cut + 1])
            for i, value in enumerate(((mine + other), mine, other)):
                value = value.astype(BF)
                for side in range(2):
                    at = piece * 256 + side * L
                    glu[i * L : (i + 1) * L, at : at + L] = value[side * L : (side + 1) * L, :]
        sums = nt(glu[0:L, :], glu[...])
        if cut == 1:
            for d in range(B):
                rows = slice(d * L, (d + 1) * L)
                value = nt(corners[2], et_own[1, rows, :]) + nt(corners[3], et_near[1, rows, :])
                inter[pl.ds(d, CHI, stride=B), :] = value[0:CHI, :]
        m = polar_right(sums[:, 0:L])
        new_own = unit_corner(product(m, sums[:, L : 2 * L]))
        if step < STEPS - 1:
            c_send[2 * cut] = new_own
            c_send[2 * cut + 1] = unit_corner(product(m, sums[:, 2 * L : 3 * L]))
            corner_send(cut).start()
        else:
            c_fin[cut] = new_own[0:CHI, 0:CHI]
        m_rows = jnp.concatenate(list(split(m)), axis=0)
        if cut == 0:
            for piece in range(8):
                both = nn(m_rows, glu[0:L, piece * 256 : (piece + 1) * 256])
                both = (both[0:L] + both[L : 2 * L]).astype(BF)
                for side in range(2):
                    at = piece * 256 + side * L
                    pt[at : at + L, :] = both[:, side * L : (side + 1) * L]
        else:
            for piece in range(6):
                rows = slice(piece * 256, (piece + 1) * 256)
                both = nt(m_rows, inter[rows, :].astype(BF))
                pup[:, rows] = (both[0:CHI] + both[L : L + CHI]).astype(BF)

    def contract(left, arrivals=None):
        def spread_rows(k):
            if arrivals is not None and k % 2 == 0:
                arrivals[k // 2].wait_recv()
            rows = left[k * 256 : (k + 1) * 256, :]
            for pair in range(8):
                out = nt(rows, pt[pair * 256 : (pair + 1) * 256, :]).astype(BF)
                fs[k, 2 * pair] = out[:, 0:L]
                fs[k, 2 * pair + 1] = out[:, L : 2 * L]

        def absorb(k):
            for pair in range(8):
                cols = [
                    jnp.concatenate([fs[k, d, u * B : (u + 1) * B, :] for d in range(B)], axis=0)
                    for u in (2 * pair, 2 * pair + 1)
                ]
                out = nn(w_ref[...], jnp.concatenate(cols, axis=1)).astype(BF)
                for side in range(2):
                    at = k * 256 + (2 * pair + side) * B
                    for r in range(B):
                        t_ref[r // 2, at : at + B, (r % 2) * L : (r % 2 + 1) * L] = out[
                            r * B : (r + 1) * B, side * L : (side + 1) * L
                        ]

        spread_rows(0)
        for k in range(6):
            if k < 5:
                spread_rows(k + 1)
            absorb(k)

    def close(store):
        square = jnp.zeros((CHI, CHI), F32)
        for pair in range(8):
            out = nn(pup[...], t_ref[pair])
            for side in range(2):
                value = out[:, side * L : side * L + CHI]
                square = square + value * value
                store(2 * pair + side, jnp.concatenate([value, jnp.zeros((CHI, L - CHI), F32)], axis=1))
        return lax.rsqrt(jnp.sum(square) * (1.0 / (CHI * CHI * B)) + 1e-06)

    chain(0, 0)
    contract(west)

    @pl.when(edge_row)
    def _():
        chain(1, 0)

    if spread:
        @pl.when(first & (half == 0))
        def _():
            pl.semaphore_wait(ready, 1)
            first_sends[2].start()

        @pl.when(last & (half == 0))
        def _():
            pl.semaphore_wait(ready, 1)
            first_sends[3].start()

    if spread:
        @pl.when(helper & (half == 0))
        def _():
            forward()

    chain(0, 1)

    def store_west(r, value):
        inter[pl.ds(r, CHI, stride=B), :] = value

    scale = close(store_west)
    west_shift = []
    for k in range(3):
        rows = pl.ds(k * 512, 512)
        west_send[rows, :] = (inter[rows, :] * scale).astype(BF)
        west_shift.append(
            pltpu.make_async_remote_copy(
                src_ref=west_send.at[rows], dst_ref=west_recv.at[rows], send_sem=wsend.at[k], recv_sem=wrecv.at[k],
                device_id=east, device_id_type=MESH,
            )
        )
        west_shift[k].start()

    @pl.when(jnp.logical_not(edge_row))
    def _():
        chain(1, 0)

    chain(1, 1)
    for copy in last_corners:
        copy.start()
    contract(west_recv, west_shift)

    def store_last(r, value):
        fin[r, 0:CHI, :] = value

    scale = close(store_last)

    @pl.when(mirror)
    def _():
        e_fin[...] = jnp.concatenate([(fin[r].T[0:CHI, 0:CHI] * scale).astype(BF) for r in range(B)], axis=1)

    @pl.when(jnp.logical_not(mirror))
    def _():
        e_fin[...] = jnp.concatenate([(fin[r, 0:CHI, 0:CHI] * scale).astype(BF) for r in range(B)], axis=1)

    edge_shift = remote(e_fin, e_out.at[0, 0], 9, east)
    edge_shift.start()
    for copy in last_corners + [edge_shift]:
        copy.wait_recv()
    for copy in last_corners + west_shift + [edge_shift, corner_send(0), corner_send(1)] + first_sends[2:]:
        copy.wait_send()
    if spread:
        @pl.when(jnp.logical_not(first))
        def _():
            first_sends[0].wait_send()

        @pl.when(jnp.logical_not(last))
        def _():
            first_sends[1].wait_send()

        @pl.when(helper)
        def _():
            for copy in forwards():
                copy.wait_send()
    else:
        first_sends[0].wait_send()
        first_sends[1].wait_send()


def settle(*refs):
    sources, targets, stages, sem = refs[0:3], refs[3:6], refs[6:9], refs[9]
    fetch = [pltpu.make_async_copy(sources[i], stages[i], sem.at[i]) for i in range(3)]
    keep = [pltpu.make_async_copy(stages[i], targets[i], sem.at[3 + i]) for i in range(3)]
    for copy in fetch:
        copy.start()
    for i in (0, 2, 1):
        fetch[i].wait()
        keep[i].start()
    for copy in keep:
        copy.wait()


def per_device(c_upper, edge_upper, edge_left, c_lower, edge_lower, site_ket, time_gate, quench_sites):
    hbm = pl.BlockSpec(memory_space=pl.ANY)
    vmem = pl.BlockSpec(memory_space=pltpu.VMEM)
    smem = pl.BlockSpec(memory_space=pltpu.SMEM)
    corner = jax.ShapeDtypeStruct((1, 1, CHI, CHI), BF)
    edge = jax.ShapeDtypeStruct((1, 1, CHI, B * CHI), BF)
    inner = pltpu.VMEM((CHI * B, L), BF)
    four = pltpu.VMEM((4, L, L), BF)
    two_edges = pltpu.VMEM((2, CHI, B * CHI), BF)
    two_tall = pltpu.VMEM((2, B * L, L), BF)
    dma = pltpu.SemaphoreType.DMA
    moved = pl.pallas_call(
        kernel,
        out_shape=(corner, edge, corner),
        in_specs=[hbm] * 5 + [vmem, smem, smem],
        out_specs=(hbm,) * 3,
        scratch_shapes=[
            two_edges, two_edges, pltpu.VMEM((CHI, B * CHI), BF), pltpu.VMEM((4, CHI, CHI), BF),
            two_tall, two_tall, four, four, four, pltpu.VMEM((256, 256), BF),
            inner, inner, inner, pltpu.VMEM((3 * L, B * L), BF), pltpu.VMEM((CHI * B, L), F32),
            pltpu.VMEM((CHI, CHI * B), BF), pltpu.VMEM((B * L, L), BF), pltpu.VMEM((6, B, 256, L), BF),
            pltpu.VMEM((8, CHI * B, 2 * L), BF), pltpu.VMEM((B, L, L), F32),
            pltpu.VMEM((CHI, B * CHI), BF), pltpu.VMEM((2, CHI, CHI), BF),
            pltpu.VMEM((2, CHI, L), BF),
            dma((5,)), dma((10,)), dma((10,)), dma((CHUNKS,)), dma((2,)), dma((3,)), dma((3,)),
            pltpu.SemaphoreType.REGULAR,
        ],
        compiler_params=pltpu.CompilerParams(
            collective_id=0, has_side_effects=True, vmem_limit_bytes=63 * 1024 * 1024
        ),
        name="left_move",
    )(c_upper, edge_upper, edge_left, c_lower, edge_lower, site_ket, time_gate, quench_sites)
    return pl.pallas_call(
        settle,
        out_shape=(corner, edge, corner),
        in_specs=[hbm] * 3,
        out_specs=(hbm,) * 3,
        scratch_shapes=[
            pltpu.VMEM((1, 1, CHI, CHI), BF), pltpu.VMEM((1, 1, CHI, B * CHI), BF), pltpu.VMEM((1, 1, CHI, CHI), BF),
            pltpu.SemaphoreType.DMA((6,)),
        ],
        compiler_params=pltpu.CompilerParams(vmem_limit_bytes=63 * 1024 * 1024),
        name="settle",
    )(*moved)


def solution(mesh):
    site = P("gx", "gy", None, None)
    return jax.shard_map(
        per_device,
        mesh=mesh,
        in_specs=(site,) * 6 + (P(), P()),
        out_specs=(site,) * 3,
        check_vma=False,
    )
```
